512 devices in a mesh: group: 16 (over y_hi, x, core), dev: 32 (over z, y_lo).
Axes of the slice: x: 4, y: 4 (y_hi: 2, y_lo: 2; y = y_hi * 2 + y_lo), z: 16, core: 2. Of those that a mesh axis runs over, the one named last changes fastest.
Arguments:
- user_feat: bfloat16 [65536, 1024], P(('group', 'dev')), may hold values from -6 to 6
- item_feat: bfloat16 [65536, 1024], P(('group', 'dev')), may hold values from -6 to 6
- item_ids: int32 [65536], P(('group', 'dev')), may hold values from 0 to 1048575
- corpus_feat: bfloat16 [131072, 1024], P(('group', 'dev')), may hold values from -6 to 6
- neg_owner: int32 [262144, 1], P(('group', 'dev')), may hold values from 0 to 31; in each aligned block of 512 rows (0 to 511, 512 to 1023, ...) at most 48 rows name the same one
- neg_row: int32 [262144], P(('group', 'dev')), may hold values from 0 to 255
- user_weight: bfloat16 [1024, 256], replicated, may hold values from -0.1875 to 0.1875
- item_weight: bfloat16 [1024, 256], replicated, may hold values from -0.1875 to 0.1875
Outputs:
- loss: float32 [65536], P(('group', 'dev'))
- grad_user: float32 [1024, 256], replicated
- grad_item: float32 [1024, 256], replicated
The draws below stay inside these ranges and needn't reach their ends.
Inputs may be any that keep to these rules, and one draw needn't show every extreme that they name: `neg_owner`: among the 512 samples of one device, no owner is named more than 48 times, a bound that some block reaches.
All inputs are finite; a program needn't handle non-finite values.
Results may differ from the reference program's by a relative error of at most 0.00075.
The reference program's roundings to bfloat16 on the way count: a program that leaves them out, or rounds other values in their place, can miss the bound.
Values may be sent and summed in bfloat16 or wider, within the bound.
A program may use at most 64 MiB of HBM per device.

```python
import math
import jax
import jax.numpy as jnp
import numpy as np
from jax import lax

D = 1024
E = 256
VOCAB = 1048576
TOK_DEV = 128
NEG_DEV = 512
CORP_DEV = 256
CAP = 48
PAIRS = 65536
SAMPLES = 262144
CORPUS = 131072
N_GROUP = 16
N_DEV = 32


def plant(result, stream_key, low, high):
    spot = [jax.random.randint(jax.random.fold_in(stream_key, axis), (), 0, length) for axis, length in enumerate(result.shape)]
    main_axis = result.shape.index(max(result.shape))
    next_to = spot[:main_axis] + [(spot[main_axis] + 1) % result.shape[main_axis]] + spot[main_axis + 1:]
    return result.at[tuple(spot)].set(low).at[tuple(next_to)].set(high)


def steps_of(own_key, shape, split, smallest, high):
    gain, own = 1.0, jax.random.fold_in(own_key, 6)
    for axis_at, shards_of in split:
        draws = jnp.exp(jax.random.uniform(jax.random.fold_in(own, axis_at), (shards_of,), jnp.float32, smallest / len(split), high / len(split)))
        gain = gain * jnp.repeat(draws, shape[axis_at] // shards_of).reshape([-1 if axis == axis_at else 1 for axis in range(len(shape))])
    return gain


def ranked_wide(own_key, extent, number_of, lean):
    portions = [min(1 << octave, number_of + 1 - (1 << octave)) * (1 << 20) // math.isqrt((1 << octave) ** lean) + 1 for octave in range((number_of + 1).bit_length()) if 1 << octave <= number_of]
    width = 1 + sum(portions) // (1 << 30)
    grid = np.cumsum(np.array([max(1, weight // width) for weight in portions]))
    pick = jax.random.randint(jax.random.fold_in(own_key, 1), extent, 0, int(grid[len(portions) - 1]))
    start = jnp.left_shift(1, jnp.searchsorted(jnp.asarray(grid, jnp.int32), pick, side="right").astype(jnp.int32))
    standing = start - 1 + jax.random.randint(jax.random.fold_in(own_key, 4), extent, 0, 1 << 30) % jnp.minimum(start, number_of + 1 - start)
    return jax.random.permutation(jax.random.fold_in(own_key, 2), number_of)[standing].astype(jnp.int32)


def deal_out(key, own, number, rows, amount, top, reach, slope):
    sequence = jax.random.permutation(key, amount)
    crowded, ordinary = portions_of(amount, rows * top, reach, slope, True), portions_of(amount, rows * top, reach, slope, False)
    places = jnp.arange(amount)

    def named(tallies, offset_by):
        used = int((tallies > 0).sum())
        fixed = max(1, used // 4)
        moved = fixed + (places - fixed + offset_by * (used - fixed)) % max(1, amount - fixed)
        return jnp.zeros((amount,), jnp.int32).at[sequence[jnp.where(places < fixed, places, moved)]].set(jnp.asarray(tallies, jnp.int32))

    tallies = jnp.where(number % 4 == 0, named(crowded, number // 4), named(ordinary, number - number // 4 - 1))
    mixed = jax.random.permutation(jax.random.fold_in(own, 3), amount)
    giver, receiver = mixed[0:amount // 2 * 2:2], mixed[1:amount // 2 * 2:2]
    slack = jnp.minimum(tallies[giver] - 1, reach - tallies[receiver]) // 2
    slack = jnp.where((giver == sequence[0]) | (receiver == sequence[0]) | (tallies[receiver] == 0), 0, jnp.maximum(slack, 0))
    moved = jax.random.randint(jax.random.fold_in(own, 4), (amount // 2,), 0, 1 << 20) % (slack + 1)
    tallies = tallies.at[giver].add(-moved).at[receiver].add(moved)
    labels = jnp.searchsorted(jnp.cumsum(tallies), jnp.arange(rows * top), side="right").astype(jnp.int32)
    grid = labels.reshape(top, rows).T
    grid = grid[jax.random.permutation(jax.random.fold_in(own, 1), rows)]
    offset_by = jax.random.randint(jax.random.fold_in(own, 2), (rows, 1), 0, top)
    return jnp.take_along_axis(grid, (jnp.arange(top)[None, :] + offset_by) % top, axis=1)


def portions_of(count, total, limit, slope, full):
    portions = [(1 << 20) // math.isqrt(standing ** slope) + 1 for standing in range(1, count + 1)]
    largest = limit if full else min(limit, max(-(-total // count), total * portions[0] // sum(portions)))
    least = 1 if total - largest >= count - 1 else 0
    given, surplus = [largest] + [least] * (count - 1), total - largest - least * (count - 1)
    while surplus > 0:
        candidates = [i for i in range(1, count) if given[i] < largest] or [i for i in range(1, count) if given[i] < limit]
        pool, left = sum([portions[i] for i in candidates]), surplus
        for i in candidates:
            addition = min(limit - given[i], max(1, left * portions[i] // pool), surplus)
            given[i] = given[i] + addition
            surplus = surplus - addition
    return np.array(given)


def bell_draw(key, shape, deviation, most, pieces=(), kind=jnp.bfloat16):
    level = steps_of(key, shape, pieces, -0.22, 0.18) if pieces else 1.0
    array = jax.random.normal(key, shape, jnp.float32) * deviation * level
    return jnp.minimum(jnp.maximum(array, -most), most).astype(kind)


def setup_inputs(seed: int = 0) -> dict:
    key_list = jax.random.split(jax.random.key(seed), 9)
    user_feat = bell_draw(key_list[0], (PAIRS, D), 1.0, 6.0, ((0, 512),))
    item_feat = bell_draw(key_list[1], (PAIRS, D), 1.0, 6.0, ((0, 512),))
    item_ids = plant(ranked_wide(key_list[2], (PAIRS,), VOCAB, 2), jax.random.fold_in(key_list[2], 3), 0, VOCAB - 1).astype(jnp.int32)
    corpus_feat = bell_draw(key_list[3], (CORPUS, D), 1.0, 6.0, ((0, 512),))
    neg_owner_keys = jax.random.split(jax.random.fold_in(key_list[4], 1), SAMPLES // NEG_DEV)
    neg_owner_turns = jax.random.permutation(jax.random.fold_in(key_list[4], 3), SAMPLES // NEG_DEV)
    neg_owner = jax.vmap(lambda own, number: deal_out(jax.random.fold_in(key_list[4], 2), own, number, NEG_DEV, N_DEV, 1, CAP, 2))(neg_owner_keys, neg_owner_turns).reshape((SAMPLES, 1))
    neg_row = plant(jax.random.randint(key_list[5], (SAMPLES,), 0, CORP_DEV), jax.random.fold_in(key_list[5], 1), 0, CORP_DEV - 1).astype(jnp.int32)
    user_weight = bell_draw(key_list[6], (D, E), D ** -0.5, 0.1875)
    item_weight = bell_draw(key_list[7], (D, E), D ** -0.5, 0.1875)
    return {"user_feat": user_feat, "item_feat": item_feat, "item_ids": item_ids, "corpus_feat": corpus_feat, "neg_owner": neg_owner, "neg_row": neg_row, "user_weight": user_weight, "item_weight": item_weight}


sharpen = 20.0
epsilon = 1e-06

def project(features, weight):
    hidden = jnp.dot(features, weight, preferred_element_type=jnp.float32)
    inverse = lax.rsqrt(lax.optimization_barrier(jnp.sum(hidden * hidden, axis=-1, keepdims=True)) + epsilon)
    return (hidden * inverse, inverse)

def unnormalize(unit, inverse, upstream):
    along = lax.optimization_barrier(jnp.sum(unit * upstream, axis=-1, keepdims=True))
    return ((upstream - unit * along) * inverse).astype(jnp.bfloat16)

def reference(user_feat, item_feat, item_ids, corpus_feat, neg_owner, neg_row, user_weight, item_weight):
    users = user_feat.reshape(N_GROUP, N_DEV, TOK_DEV, D)
    items = item_feat.reshape(N_GROUP, N_DEV, TOK_DEV, D)
    id_table = item_ids.reshape(N_GROUP, N_DEV, TOK_DEV)
    owners = neg_owner.reshape(N_GROUP, N_DEV, NEG_DEV)
    rows_within = neg_row.reshape(N_GROUP, N_DEV, NEG_DEV)
    group_base = jnp.arange(N_GROUP, dtype=jnp.int32)[:, None, None] * N_DEV
    corpus_index = ((group_base + owners) * CORP_DEV + rows_within).astype(jnp.int32)
    cycle_size = N_GROUP * TOK_DEV
    columns = jnp.arange(cycle_size, dtype=jnp.int32)
    diagonal = columns[:, None] == columns[None, :]
    factor = sharpen / TOK_DEV

    def one_column(carry, index):
        grad_user, grad_item = carry
        user_rows = lax.dynamic_index_in_dim(users, index, 1, keepdims=False).reshape(cycle_size, D)
        item_rows = lax.dynamic_index_in_dim(items, index, 1, keepdims=False).reshape(cycle_size, D)
        cycle_ids = lax.dynamic_index_in_dim(id_table, index, 1, keepdims=False).reshape(cycle_size)
        sample_index = lax.dynamic_index_in_dim(corpus_index, index, 1, keepdims=False).reshape(-1)
        sample_feat = corpus_feat[sample_index]
        user_unit, user_inv = project(user_rows, user_weight)
        user_low = user_unit.astype(jnp.bfloat16)
        item_unit, item_inv = project(item_rows, item_weight)
        item_low = item_unit.astype(jnp.bfloat16)
        sample_unit, sample_inv = project(sample_feat, item_weight)
        sample_low = sample_unit.astype(jnp.bfloat16)
        user_wide = user_low.astype(jnp.float32).reshape(N_GROUP, TOK_DEV, E)
        sample_wide = sample_low.astype(jnp.float32).reshape(N_GROUP, NEG_DEV, E)
        cycle_logit = sharpen * jnp.dot(user_low, item_low.T, preferred_element_type=jnp.float32)
        sample_logit = sharpen * jnp.einsum('gte,gne->gtn', user_wide, sample_wide).reshape(cycle_size, NEG_DEV)
        keep = jnp.logical_not((cycle_ids[:, None] == cycle_ids[None, :]) & jnp.logical_not(diagonal))
        cycle_exp = jnp.where(keep, jnp.exp(cycle_logit), jnp.float32(0.0))
        sample_exp = jnp.exp(sample_logit)
        total = lax.optimization_barrier(jnp.sum(cycle_exp, axis=1)) + lax.optimization_barrier(jnp.sum(sample_exp, axis=1))
        loss = jnp.log(total) - jnp.diagonal(cycle_logit)
        cycle_grad = ((cycle_exp / total[:, None] - diagonal.astype(jnp.float32)) * factor).astype(jnp.bfloat16)
        sample_grad = (sample_exp / total[:, None] * factor).astype(jnp.bfloat16)
        sample_grad_wide = sample_grad.astype(jnp.float32).reshape(N_GROUP, TOK_DEV, NEG_DEV)
        user_up = jnp.dot(cycle_grad, item_low, preferred_element_type=jnp.float32) + jnp.einsum('gtn,gne->gte', sample_grad_wide, sample_wide).reshape(cycle_size, E)
        item_up = jnp.dot(cycle_grad.T, user_low, preferred_element_type=jnp.float32)
        sample_up = jnp.einsum('gtn,gte->gne', sample_grad_wide, user_wide).reshape(N_GROUP * NEG_DEV, E)
        user_back = unnormalize(user_unit, user_inv, user_up)
        item_back = unnormalize(item_unit, item_inv, item_up)
        sample_back = unnormalize(sample_unit, sample_inv, sample_up)
        grad_user = grad_user + jnp.dot(user_rows.T, user_back, preferred_element_type=jnp.float32)
        grad_item = grad_item + jnp.dot(item_rows.T, item_back, preferred_element_type=jnp.float32) + jnp.dot(sample_feat.T, sample_back, preferred_element_type=jnp.float32)
        return ((grad_user, grad_item), loss)
    start = (jnp.zeros((D, E), jnp.float32), jnp.zeros((D, E), jnp.float32))
    (grad_user, grad_item), losses = lax.scan(one_column, start, jnp.arange(N_DEV, dtype=jnp.int32))
    loss = losses.reshape(N_DEV, N_GROUP, TOK_DEV).transpose(1, 0, 2).reshape(-1)
    return (loss, grad_user, grad_item)
```

```python
import jax
import jax.numpy as jnp
from jax import lax
from jax.experimental import pallas as pl
from jax.experimental.pallas import tpu as pltpu
from jax.sharding import PartitionSpec as P

sharpen = 20.0
epsilon = 1e-06
MESH = pl.DeviceIdType.MESH
NX, NY, NZ = 4, 4, 16


def place():
    group, dev = lax.axis_index("group"), lax.axis_index("dev")
    core, x, y_hi = group % 2, (group // 2) % NX, group // (2 * NX)
    z, y_lo = dev // 2, dev % 2
    return core, x, y_hi * 2 + y_lo, z


def device_at(core, x, y, z):
    return (((y // 2) * NX + x) * 2 + core, z * 2 + y % 2)


def greet(partners):
    barrier = pltpu.get_barrier_semaphore()
    for partner in partners:
        pl.semaphore_signal(barrier, inc=1, device_id=partner, device_id_type=MESH)
    pl.semaphore_wait(barrier, len(partners))


def remote(src, dst, send_sem, recv_sem, device):
    return pltpu.make_async_remote_copy(
        src_ref=src, dst_ref=dst, send_sem=send_sem, recv_sem=recv_sem, device_id=device, device_id_type=MESH
    )


HALF = 1024
FOLD = 512
PART = 128
BIT = 32


def reduce_all_kernel(
    user_ref, item_ref, out_ref, mine, from_core, from_first, from_second, from_z, load_sem,
    core_send, core_recv, first_send, first_recv, second_send, second_recv, z_send, z_recv,
    zg_send, zg_recv, sg_send, sg_recv, fg_send, fg_recv, cg_send, cg_recv,
):
    core, x, y, z = place()
    other = 1 - core
    sibling = device_at(other, x, y, z)
    loads = [
        pltpu.make_async_copy(user_ref, mine.at[0], load_sem.at[0]),
        pltpu.make_async_copy(item_ref, mine.at[1], load_sem.at[1]),
    ]
    for load in loads:
        load.start()
    along = [
        [device_at(core, (x + k) % NX, y, z) for k in range(1, NX)],
        [device_at(core, x, (y + k) % NY, z) for k in range(1, NY)],
    ]
    along_z = [device_at(core, x, y, (z + k) % NZ) for k in range(1, NZ)]
    greet([sibling] + along[0] + along[1] + along_z)
    for load in loads:
        load.wait()
    first_at, second_at = [x, y], [y, x]

    def part_rows(fold, part):
        return pl.ds(pl.multiple_of(fold * FOLD + part * PART, PART), PART)

    def bit_rows(fold, part, bit):
        return pl.ds(pl.multiple_of(fold * FOLD + part * PART + bit * BIT, BIT), BIT)

    def tile_of(at):
        fold = at // 8
        part = x + fold * (y - x)
        bit = y + fold * (x - y)
        row = fold * FOLD + part * PART + bit * BIT + ((at // 2) % 4) * 8
        return pl.ds(pl.multiple_of(row, 8), 8), pl.ds(pl.multiple_of((at % 2) * 128, 128), 128)

    order = [(k, fold) for k in (1, 2, 3, 0) for fold in (0, 1)]
    core_copies = []
    for n, (k, fold) in enumerate(order):
        rows = part_rows(fold, (first_at[fold] + k) % 4)
        copy = remote(mine.at[other, rows], from_core.at[n], core_send.at[n], core_recv.at[n], sibling)
        copy.start()
        core_copies.append(copy)
    first_copies = []
    for n, (k, fold) in enumerate(order):
        rows = part_rows(fold, (first_at[fold] + k) % 4)
        core_copies[n].wait_recv()
        mine[core, rows] += from_core[n]
        if k:
            copy = remote(
                mine.at[core, rows], from_first.at[fold, k - 1], first_send.at[fold, k - 1],
                first_recv.at[fold, k - 1], along[fold][k - 1],
            )
            copy.start()
            first_copies.append((copy, k, fold))
    for copy, k, fold in first_copies:
        copy.wait_recv()
    second_copies = []
    for k in (1, 2, 3, 0):
        for fold in (0, 1):
            at = (second_at[fold] + k) % 4
            rows = bit_rows(fold, first_at[fold], at)
            near = pl.ds(pl.multiple_of(at * BIT, BIT), BIT)
            mine[core, rows] += from_first[fold, 0, near] + from_first[fold, 1, near] + from_first[fold, 2, near]
            if k:
                copy = remote(
                    mine.at[core, rows], from_second.at[fold, k - 1], second_send.at[fold, k - 1],
                    second_recv.at[fold, k - 1], along[1 - fold][k - 1],
                )
                copy.start()
                second_copies.append((copy, k, fold))
    for copy, k, fold in second_copies:
        copy.wait_recv()
    for fold in (0, 1):
        rows = bit_rows(fold, first_at[fold], second_at[fold])
        mine[core, rows] += from_second[fold, 0] + from_second[fold, 1] + from_second[fold, 2]
    z_copies = []
    for k in range(1, NZ):
        rows, columns = tile_of((z + k) % NZ)
        copy = remote(
            mine.at[core, rows, columns], from_z.at[k - 1], z_send.at[k - 1], z_recv.at[k - 1], along_z[k - 1]
        )
        copy.start()
        z_copies.append(copy)
    rows, columns = tile_of(z)
    total = mine[core, rows, columns]
    for k, copy in enumerate(z_copies):
        copy.wait_recv()
        total = total + from_z[k]
    out_ref[core, rows, columns] = total
    gathers = []
    for k in range(1, NZ):
        tile = out_ref.at[core, rows, columns]
        copy = remote(tile, tile, zg_send.at[k - 1], zg_recv.at[k - 1], along_z[k - 1])
        copy.start()
        gathers.append(copy)
    for k in range(1, NZ):
        tile_rows, tile_columns = tile_of((z + NZ - k) % NZ)
        tile = out_ref.at[core, tile_rows, tile_columns]
        remote(tile, tile, zg_send.at[k - 1], zg_recv.at[k - 1], along_z[k - 1]).wait_recv()
    for k in (1, 2, 3):
        for fold in (0, 1):
            bit = out_ref.at[core, bit_rows(fold, first_at[fold], second_at[fold])]
            copy = remote(bit, bit, sg_send.at[fold, k - 1], sg_recv.at[fold, k - 1], along[1 - fold][k - 1])
            copy.start()
            gathers.append(copy)
    for k in (1, 2, 3):
        for fold in (0, 1):
            bit = out_ref.at[core, bit_rows(fold, first_at[fold], (second_at[fold] + 4 - k) % 4)]
            remote(bit, bit, sg_send.at[fold, k - 1], sg_recv.at[fold, k - 1], along[1 - fold][k - 1]).wait_recv()
    for k in (1, 2, 3):
        for fold in (0, 1):
            part = out_ref.at[core, part_rows(fold, first_at[fold])]
            copy = remote(part, part, fg_send.at[fold, k - 1], fg_recv.at[fold, k - 1], along[fold][k - 1])
            copy.start()
            gathers.append(copy)
    for k in (0, 1, 2, 3):
        for fold in (0, 1):
            rows = part_rows(fold, (first_at[fold] + 4 - k) % 4)
            part = out_ref.at[core, rows]
            if k:
                remote(part, part, fg_send.at[fold, k - 1], fg_recv.at[fold, k - 1], along[fold][k - 1]).wait_recv()
            copy = remote(part, part, cg_send.at[fold, k], cg_recv.at[fold, k], sibling)
            copy.start()
            gathers.append(copy)
    for k in (0, 1, 2, 3):
        for fold in (0, 1):
            part = out_ref.at[other, part_rows(fold, (first_at[fold] + 4 - k) % 4)]
            remote(part, part, cg_send.at[fold, k], cg_recv.at[fold, k], sibling).wait_recv()
    for copy in core_copies + [c for c, _, _ in first_copies + second_copies] + z_copies + gathers:
        copy.wait_send()


def reduce_all(grad_user, grad_item):
    dma = pltpu.SemaphoreType.DMA
    out = pl.pallas_call(
        reduce_all_kernel,
        out_shape=jax.ShapeDtypeStruct((2, HALF, 256), jnp.float32),
        in_specs=[pl.BlockSpec(memory_space=pl.ANY)] * 2,
        out_specs=pl.BlockSpec(memory_space=pltpu.VMEM),
        scratch_shapes=[
            pltpu.VMEM((2, HALF, 256), jnp.float32),
            pltpu.VMEM((8, PART, 256), jnp.float32),
            pltpu.VMEM((2, 3, PART, 256), jnp.float32),
            pltpu.VMEM((2, 3, BIT, 256), jnp.float32),
            pltpu.VMEM((NZ - 1, 8, 128), jnp.float32),
            dma((2,)),
            dma((8,)), dma((8,)), dma((2, 3)), dma((2, 3)), dma((2, 3)), dma((2, 3)), dma((NZ - 1,)), dma((NZ - 1,)),
            dma((NZ - 1,)), dma((NZ - 1,)), dma((2, 3)), dma((2, 3)), dma((2, 3)), dma((2, 3)), dma((2, 4)), dma((2, 4)),
        ],
        compiler_params=pltpu.CompilerParams(
            collective_id=0, has_side_effects=True, vmem_limit_bytes=24 * 1024 * 1024
        ),
        name="reduce_all",
    )(grad_user, grad_item)
    return out[0], out[1]

def project(features, weight):
    hidden = jnp.dot(features, weight, preferred_element_type=jnp.float32)
    inverse = lax.rsqrt(jnp.sum(hidden * hidden, axis=-1, keepdims=True) + epsilon)
    return (hidden * inverse, inverse)


def unnormalize(unit, inverse, upstream):
    along = jnp.sum(unit * upstream, axis=-1, keepdims=True)
    return ((upstream - unit * along) * inverse).astype(jnp.bfloat16)


def contract(left, right, left_dim, right_dim):
    return lax.dot_general(
        left, right, (((left_dim,), (right_dim,)), ((), ())), preferred_element_type=jnp.float32
    )


def local(
    user_feat, item_feat, item_ids, corpus_feat, neg_owner, neg_row, user_weight, item_weight
):
    tok_rows = user_feat.shape[0]
    owner_count = lax.axis_size("dev")
    sample_count = neg_row.shape[0]
    capacity = 3 * sample_count // owner_count
    width = user_weight.shape[1]
    owned_rows = corpus_feat.shape[0]
    factor = sharpen / tok_rows
    user_unit, user_inv = project(user_feat, user_weight)
    user_low = user_unit.astype(jnp.bfloat16)
    item_unit, item_inv = project(item_feat, item_weight)
    item_low = item_unit.astype(jnp.bfloat16)
    cycle_items, cycle_ids = (
        lax.all_gather(item_low, "group", axis=0, tiled=True),
        lax.all_gather(item_ids, "group", axis=0, tiled=True),
    )
    owners = neg_owner[:, 0]
    owner_hot = (owners[:, None] == jnp.arange(owner_count, dtype=jnp.int32)[None, :]).astype(
        jnp.int32
    )
    earlier = jnp.cumsum(owner_hot, axis=0) - owner_hot
    slot = owners * capacity + jnp.sum(earlier * owner_hot, axis=1)
    wanted = jnp.full((owner_count * capacity,), -1, jnp.int32).at[slot].set(neg_row)
    requests = lax.all_to_all(
        wanted.reshape(owner_count, capacity), "dev", split_axis=0, concat_axis=0, tiled=True
    ).reshape(-1)
    valid = requests >= 0
    safe_rows = jnp.where(valid, requests, 0)
    corpus_unit, corpus_inv = project(corpus_feat, item_weight)
    reply = corpus_unit.astype(jnp.bfloat16)[safe_rows].reshape(owner_count, capacity, width)
    arrived = lax.all_to_all(reply, "dev", split_axis=0, concat_axis=0, tiled=True).reshape(
        owner_count * capacity, width
    )
    sample_low = arrived[slot]
    cycle_logit = sharpen * contract(user_low, cycle_items, 1, 1)
    sample_logit = sharpen * contract(user_low, sample_low, 1, 1)
    columns = jnp.arange(cycle_ids.shape[0], dtype=jnp.int32)
    here = lax.axis_index("group")
    own_column = here * tok_rows + jnp.arange(tok_rows, dtype=jnp.int32)
    diagonal = columns[None, :] == own_column[:, None]
    keep = jnp.logical_not((cycle_ids[None, :] == item_ids[:, None]) & jnp.logical_not(diagonal))
    cycle_exp = jnp.where(keep, jnp.exp(cycle_logit), jnp.float32(0.0))
    sample_exp = jnp.exp(sample_logit)
    total = jnp.sum(cycle_exp, axis=1) + jnp.sum(sample_exp, axis=1)
    own_logit = jnp.sum(jnp.where(diagonal, cycle_logit, jnp.float32(0.0)), axis=1)
    loss = jnp.log(total) - own_logit
    cycle_grad = ((cycle_exp / total[:, None] - diagonal.astype(jnp.float32)) * factor).astype(
        jnp.bfloat16
    )
    sample_grad = (sample_exp / total[:, None] * factor).astype(jnp.bfloat16)
    user_up = jnp.dot(cycle_grad, cycle_items, preferred_element_type=jnp.float32) + jnp.dot(
        sample_grad, sample_low, preferred_element_type=jnp.float32
    )
    item_up = lax.psum_scatter(
        contract(cycle_grad, user_low, 0, 0), "group", scatter_dimension=0, tiled=True
    )
    sample_up = contract(sample_grad, user_low, 0, 0)
    placed = jnp.zeros((owner_count * capacity, width), jnp.float32).at[slot].set(sample_up)
    returned = lax.all_to_all(
        placed.reshape(owner_count, capacity, width), "dev", split_axis=0, concat_axis=0, tiled=True
    ).reshape(owner_count * capacity, width)
    slot_back = unnormalize(corpus_unit[safe_rows], corpus_inv[safe_rows], returned)
    owner_table = (
        (jnp.arange(owned_rows, dtype=jnp.int32)[:, None] == requests[None, :]) & valid[None, :]
    ).astype(jnp.bfloat16)
    owned_back = jnp.dot(owner_table, slot_back, preferred_element_type=jnp.float32)
    corpus_grad = lax.dot_general(
        corpus_feat.astype(jnp.float32),
        owned_back,
        (((0,), (0,)), ((), ())),
        precision=lax.Precision.HIGHEST,
        preferred_element_type=jnp.float32,
    )
    user_back = unnormalize(user_unit, user_inv, user_up)
    item_back = unnormalize(item_unit, item_inv, item_up)
    grad_user = contract(user_feat, user_back, 0, 0)
    grad_item = contract(item_feat, item_back, 0, 0) + corpus_grad
    grad_user, grad_item = reduce_all(grad_user, grad_item)
    return (loss, grad_user, grad_item)


def solution(mesh):
    return jax.shard_map(
        local,
        mesh=mesh,
        in_specs=(
            P(("group", "dev"), None),
            P(("group", "dev"), None),
            P(("group", "dev")),
            P(("group", "dev"), None),
            P(("group", "dev"), None),
            P(("group", "dev")),
            P(),
            P(),
        ),
        out_specs=(P(("group", "dev")), P(), P()),
        check_vma=False,
    )
```

```python
import jax
import jax.numpy as jnp
from jax import lax
from jax.experimental import pallas as pl
from jax.experimental.pallas import tpu as pltpu
from jax.sharding import PartitionSpec as P

sharpen = 20.0
epsilon = 1e-06
MESH = pl.DeviceIdType.MESH
NX, NY, NZ = 4, 4, 16


def place():
    group, dev = lax.axis_index("group"), lax.axis_index("dev")
    core, x, y_hi = group % 2, (group // 2) % NX, group // (2 * NX)
    z, y_lo = dev // 2, dev % 2
    return core, x, y_hi * 2 + y_lo, z


def device_at(core, x, y, z):
    return (((y // 2) * NX + x) * 2 + core, z * 2 + y % 2)


def greet(partners):
    barrier = pltpu.get_barrier_semaphore()
    for partner in partners:
        pl.semaphore_signal(barrier, inc=1, device_id=partner, device_id_type=MESH)
    pl.semaphore_wait(barrier, len(partners))


def remote(src, dst, send_sem, recv_sem, device):
    return pltpu.make_async_remote_copy(
        src_ref=src, dst_ref=dst, send_sem=send_sem, recv_sem=recv_sem, device_id=device, device_id_type=MESH
    )


HALF = 1024
FOLD = 512
PART = 128
BIT = 32


def reduce_all_kernel(
    user_ref, item_ref, out_ref, mine, from_core, from_first, from_second, from_z, load_sem,
    core_send, core_recv, first_send, first_recv, second_send, second_recv, z_send, z_recv,
    zg_send, zg_recv, sg_send, sg_recv, fg_send, fg_recv, cg_send, cg_recv,
):
    core, x, y, z = place()
    other = 1 - core
    sibling = device_at(other, x, y, z)
    loads = [
        pltpu.make_async_copy(user_ref, mine.at[0], load_sem.at[0]),
        pltpu.make_async_copy(item_ref, mine.at[1], load_sem.at[1]),
    ]
    for load in loads:
        load.start()
    along = [
        [device_at(core, (x + k) % NX, y, z) for k in range(1, NX)],
        [device_at(core, x, (y + k) % NY, z) for k in range(1, NY)],
    ]
    along_z = [device_at(core, x, y, (z + k) % NZ) for k in range(1, NZ)]
    greet([sibling] + along[0] + along[1] + along_z)
    for load in loads:
        load.wait()
    first_at, second_at = [x, y], [y, x]

    def part_rows(fold, part):
        return pl.ds(pl.multiple_of(fold * FOLD + part * PART, PART), PART)

    def bit_rows(fold, part, bit):
        return pl.ds(pl.multiple_of(fold * FOLD + part * PART + bit * BIT, BIT), BIT)

    def tile_of(at):
        fold = at // 8
        part = x + fold * (y - x)
        bit = y + fold * (x - y)
        row = fold * FOLD + part * PART + bit * BIT + ((at // 2) % 4) * 8
        return pl.ds(pl.multiple_of(row, 8), 8), pl.ds(pl.multiple_of((at % 2) * 128, 128), 128)

    order = [(k, fold) for k in (1, 2, 3, 0) for fold in (0, 1)]
    core_copies = []
    for n, (k, fold) in enumerate(order):
        rows = part_rows(fold, (first_at[fold] + k) % 4)
        copy = remote(mine.at[other, rows], from_core.at[n], core_send.at[n], core_recv.at[n], sibling)
        copy.start()
        core_copies.append(copy)
    first_copies = []
    for n, (k, fold) in enumerate(order):
        rows = part_rows(fold, (first_at[fold] + k) % 4)
        core_copies[n].wait_recv()
        mine[core, rows] += from_core[n]
        if k:
            copy = remote(
                mine.at[core, rows], from_first.at[fold, k - 1], first_send.at[fold, k - 1],
                first_recv.at[fold, k - 1], along[fold][k - 1],
            )
            copy.start()
            first_copies.append((copy, k, fold))
    for copy, k, fold in first_copies:
        copy.wait_recv()
    second_copies = []
    for k in (1, 2, 3, 0):
        for fold in (0, 1):
            at = (second_at[fold] + k) % 4
            rows = bit_rows(fold, first_at[fold], at)
            near = pl.ds(pl.multiple_of(at * BIT, BIT), BIT)
            mine[core, rows] += from_first[fold, 0, near] + from_first[fold, 1, near] + from_first[fold, 2, near]
            if k:
                copy = remote(
                    mine.at[core, rows], from_second.at[fold, k - 1], second_send.at[fold, k - 1],
                    second_recv.at[fold, k - 1], along[1 - fold][k - 1],
                )
                copy.start()
                second_copies.append((copy, k, fold))
    for copy, k, fold in second_copies:
        copy.wait_recv()
    for fold in (0, 1):
        rows = bit_rows(fold, first_at[fold], second_at[fold])
        mine[core, rows] += from_second[fold, 0] + from_second[fold, 1] + from_second[fold, 2]
    z_copies = []
    for k in range(1, NZ):
        rows, columns = tile_of((z + k) % NZ)
        copy = remote(
            mine.at[core, rows, columns], from_z.at[k - 1], z_send.at[k - 1], z_recv.at[k - 1], along_z[k - 1]
        )
        copy.start()
        z_copies.append(copy)
    rows, columns = tile_of(z)
    total = mine[core, rows, columns]
    for k, copy in enumerate(z_copies):
        copy.wait_recv()
        total = total + from_z[k]
    out_ref[core, rows, columns] = total
    gathers = []
    for k in range(1, NZ):
        tile = out_ref.at[core, rows, columns]
        copy = remote(tile, tile, zg_send.at[k - 1], zg_recv.at[k - 1], along_z[k - 1])
        copy.start()
        gathers.append(copy)
    for k in range(1, NZ):
        tile_rows, tile_columns = tile_of((z + NZ - k) % NZ)
        tile = out_ref.at[core, tile_rows, tile_columns]
        remote(tile, tile, zg_send.at[k - 1], zg_recv.at[k - 1], along_z[k - 1]).wait_recv()
    for k in (1, 2, 3):
        for fold in (0, 1):
            bit = out_ref.at[core, bit_rows(fold, first_at[fold], second_at[fold])]
            copy = remote(bit, bit, sg_send.at[fold, k - 1], sg_recv.at[fold, k - 1], along[1 - fold][k - 1])
            copy.start()
            gathers.append(copy)
    for k in (1, 2, 3):
        for fold in (0, 1):
            bit = out_ref.at[core, bit_rows(fold, first_at[fold], (second_at[fold] + 4 - k) % 4)]
            remote(bit, bit, sg_send.at[fold, k - 1], sg_recv.at[fold, k - 1], along[1 - fold][k - 1]).wait_recv()
    for k in (1, 2, 3):
        for fold in (0, 1):
            part = out_ref.at[core, part_rows(fold, first_at[fold])]
            copy = remote(part, part, fg_send.at[fold, k - 1], fg_recv.at[fold, k - 1], along[fold][k - 1])
            copy.start()
            gathers.append(copy)
    for k in (0, 1, 2, 3):
        for fold in (0, 1):
            rows = part_rows(fold, (first_at[fold] + 4 - k) % 4)
            part = out_ref.at[core, rows]
            if k:
                remote(part, part, fg_send.at[fold, k - 1], fg_recv.at[fold, k - 1], along[fold][k - 1]).wait_recv()
            copy = remote(part, part, cg_send.at[fold, k], cg_recv.at[fold, k], sibling)
            copy.start()
            gathers.append(copy)
    for k in (0, 1, 2, 3):
        for fold in (0, 1):
            part = out_ref.at[other, part_rows(fold, (first_at[fold] + 4 - k) % 4)]
            remote(part, part, cg_send.at[fold, k], cg_recv.at[fold, k], sibling).wait_recv()
    for copy in core_copies + [c for c, _, _ in first_copies + second_copies] + z_copies + gathers:
        copy.wait_send()


def reduce_all(grad_user, grad_item):
    dma = pltpu.SemaphoreType.DMA
    out = pl.pallas_call(
        reduce_all_kernel,
        out_shape=jax.ShapeDtypeStruct((2, HALF, 256), jnp.float32),
        in_specs=[pl.BlockSpec(memory_space=pl.ANY)] * 2,
        out_specs=pl.BlockSpec(memory_space=pltpu.VMEM),
        scratch_shapes=[
            pltpu.VMEM((2, HALF, 256), jnp.float32),
            pltpu.VMEM((8, PART, 256), jnp.float32),
            pltpu.VMEM((2, 3, PART, 256), jnp.float32),
            pltpu.VMEM((2, 3, BIT, 256), jnp.float32),
            pltpu.VMEM((NZ - 1, 8, 128), jnp.float32),
            dma((2,)),
            dma((8,)), dma((8,)), dma((2, 3)), dma((2, 3)), dma((2, 3)), dma((2, 3)), dma((NZ - 1,)), dma((NZ - 1,)),
            dma((NZ - 1,)), dma((NZ - 1,)), dma((2, 3)), dma((2, 3)), dma((2, 3)), dma((2, 3)), dma((2, 4)), dma((2, 4)),
        ],
        compiler_params=pltpu.CompilerParams(
            collective_id=0, has_side_effects=True, vmem_limit_bytes=24 * 1024 * 1024
        ),
        name="reduce_all",
    )(grad_user, grad_item)
    return out[0], out[1]

TOK, OWN, NEG, WIDE, E = 128, 256, 512, 1024, 256
NG, ND = 16, 32
f32, bf16 = jnp.float32, jnp.bfloat16


def dot(left, right, left_dim=1, right_dim=0):
    return lax.dot_general(left, right, (((left_dim,), (right_dim,)), ((), ())), preferred_element_type=f32)


def project(features, weight):
    hidden = dot(features, weight)
    inverse = lax.rsqrt(jnp.sum(hidden * hidden, axis=-1, keepdims=True) + epsilon)
    return hidden * inverse, inverse


def unnormalize(unit, inverse, upstream):
    along = jnp.sum(unit * upstream, axis=-1, keepdims=True)
    return ((upstream - unit * along) * inverse).astype(bf16)


def local_grads_kernel(
    user_feat, item_feat, corpus_feat, user_weight, item_weight, ids_in, codes_in,
    loss_ref, grad_user_ref, grad_item_ref,
    uf, itf, cf, uw, iw, corp, gus, cyc, ids, codes, pair_codes, tot_g, tot_d,
    select, sel_out, sel_in, cexp, unit_u, unit_i, unit_c, inv_u, inv_i, inv_c, owned,
    load_sem, ids_send, ids_recv, codes_send, codes_recv, pair_send, pair_recv, tg_send, tg_recv, td_send, td_recv,
    zc_send, zc_recv, zu_send, zu_recv, yu_send, yu_recv, ys_send, ys_recv,
    yh_send, yh_recv, x_send, x_recv, c_send, c_recv,
):
    core, x, y, z = place()
    y_hi, y_lo = y // 2, y % 2
    group, dev = lax.axis_index("group"), lax.axis_index("dev")
    factor = sharpen / TOK
    loads = [
        pltpu.make_async_copy(src, dst, load_sem.at[n])
        for n, (src, dst) in enumerate([
            (corpus_feat, cf), (item_weight, iw), (user_feat, uf), (user_weight, uw), (item_feat, itf),
            (ids_in, ids.at[group]), (codes_in, codes.at[dev]),
        ])
    ]
    for load in loads:
        load.start()
    group_peers = [(lax.rem(group + k, NG), dev) for k in range(1, NG)]
    dev_peers = [(group, lax.rem(dev + k, ND)) for k in range(1, ND)]
    sibling = device_at(1 - core, x, y, z)
    y_partner = device_at(core, x, y_hi * 2 + 1 - y_lo, z)
    y_far = device_at(core, x, (1 - y_hi) * 2 + y_lo, z)
    x_peers = [device_at(core, (x + k) % NX, y, z) for k in range(1, NX)]
    z_peers = [device_at(core, x, y, (z + 1) % NZ), device_at(core, x, y, (z + NZ - 1) % NZ)]
    sends = []

    def send(src, dst, send_sem, recv_sem, device):
        copy = remote(src, dst, send_sem, recv_sem, device)
        copy.start()
        sends.append(copy)

    def arrived(dst, send_sem, recv_sem, device):
        remote(dst, dst, send_sem, recv_sem, device).wait_recv()

    barrier = pltpu.get_barrier_semaphore()
    for partner in group_peers + dev_peers:
        pl.semaphore_signal(barrier, inc=1, device_id=partner, device_id_type=MESH)

    loads[0].wait()
    loads[1].wait()
    unit, inverse = project(cf[...], iw[...])
    unit_c[...] = unit
    inv_c[...] = inverse
    corp[z] = unit.astype(bf16).reshape(2, TOK, E)
    pl.semaphore_wait(barrier, NG - 1 + ND - 1)

    def z_send(buf, at, s, e, way, send_sem, recv_sem):
        send(buf.at[at, e], buf.at[at, e], send_sem.at[way, s - 1, e], recv_sem.at[way, s - 1, e], z_peers[way])

    def source(way, s):
        return (z + NZ - s) % NZ if way == 0 else (z + s) % NZ

    def z_step(buf, s, send_sem, recv_sem):
        for e in (0, 1):
            for way in (0, 1):
                if s == 8 and e != way:
                    continue
                at = source(way, s)
                arrived(buf.at[at, e], send_sem.at[way, s - 1, e], recv_sem.at[way, s - 1, e], z_peers[way])
                if s < 7 or (s == 7 and e == way):
                    z_send(buf, at, s + 1, e, way, send_sem, recv_sem)

    for e in (0, 1):
        for way in (0, 1):
            z_send(corp, z, 1, e, way, zc_send, zc_recv)
    loads[6].wait()
    send(codes.at[dev], pair_codes, pair_send, pair_recv, y_partner)
    for k in range(1, ND):
        send(codes.at[dev], codes.at[dev], codes_send.at[k - 1], codes_recv.at[k - 1], dev_peers[k - 1])

    loads[2].wait()
    loads[3].wait()
    unit, inverse = project(uf[...], uw[...])
    unit_u[...] = unit
    inv_u[...] = inverse
    user_low = unit.astype(bf16)
    cyc[group, 0] = user_low
    gus[z, y_lo] = user_low
    send(gus.at[z, y_lo], gus.at[z, y_lo], yu_send, yu_recv, y_partner)
    loads[4].wait()
    unit, inverse = project(itf[...], iw[...])
    unit_i[...] = unit
    inv_i[...] = inverse
    item_low = unit.astype(bf16)
    cyc[group, 1] = item_low
    far_group = lax.rem(group + NG // 2, NG)
    send(cyc.at[group], cyc.at[group], yh_send, yh_recv, y_far)
    for k in range(1, NX):
        send(cyc.at[group], cyc.at[group], x_send.at[0, k - 1], x_recv.at[0, k - 1], x_peers[k - 1])
    send(cyc.at[group], cyc.at[group], c_send.at[0, 0], c_recv.at[0, 0], sibling)
    loads[5].wait()
    for k in range(1, NG):
        send(ids.at[group], ids.at[group], ids_send.at[k - 1], ids_recv.at[k - 1], group_peers[k - 1])


    def group_of(far, k, other):
        row = y_hi + far * (1 - 2 * y_hi)
        return (row * NX + (x + NX - k) % NX) * 2 + core + other * (1 - 2 * core)

    arrived(pair_codes, pair_send, pair_recv, y_partner)
    own_codes, their_codes = codes[dev], pair_codes[...]
    code_row = jnp.concatenate(
        [own_codes[n : n + 1] for n in range(4)] + [their_codes[n : n + 1] for n in range(4)], axis=1
    )
    wide_rows = lax.broadcasted_iota(jnp.int32, (OWN, 2 * NEG), 0)

    def select_from(at):
        hot = (code_row - (at * 2 + y_lo) * OWN == wide_rows).astype(f32).astype(bf16)
        return dot(corp[at].reshape(OWN, E), hot, 0, 0)

    select[...] = select_from(z)
    for s in range(1, 9):
        z_step(corp, s, zc_send, zc_recv)
        if s == 1:
            arrived(cyc.at[far_group], yh_send, yh_recv, y_far)
            for k in range(1, NX):
                send(cyc.at[far_group], cyc.at[far_group], x_send.at[1, k - 1], x_recv.at[1, k - 1], x_peers[k - 1])
            send(cyc.at[far_group], cyc.at[far_group], c_send.at[1, 0], c_recv.at[1, 0], sibling)
        if s in (3, 5):
            far = (s - 3) // 2
            for k in range(1, NX):
                block = cyc.at[group_of(far, k, 0)]
                arrived(block, x_send.at[far, k - 1], x_recv.at[far, k - 1], x_peers[k - 1])
                send(block, block, c_send.at[far, k], c_recv.at[far, k], sibling)
        if s == 7:
            arrived(gus.at[z, 1 - y_lo], yu_send, yu_recv, y_partner)
            for e in (0, 1):
                for way in (0, 1):
                    z_send(gus, z, 1, e, way, zu_send, zu_recv)
        if s < 8:
            select[...] += select_from(source(0, s)) + select_from(source(1, s))
        else:
            select[...] += select_from(source(0, s))
    sel_out[...] = select[:, NEG:].astype(bf16)
    send(sel_out, sel_in, ys_send, ys_recv, y_partner)

    for far in (0, 1):
        for k in range(NX):
            arrived(cyc.at[group_of(far, k, 1)], c_send.at[far, k], c_recv.at[far, k], sibling)
    for k in range(1, NG):
        arrived(ids.at[lax.rem(group + NG - k, NG)], ids_send.at[k - 1], ids_recv.at[k - 1], group_peers[k - 1])

    tile_rows = lax.broadcasted_iota(jnp.int32, (TOK, TOK), 0)
    tile_columns = lax.broadcasted_iota(jnp.int32, (TOK, TOK), 1)
    eye = tile_rows == tile_columns

    def to_row(column):
        return jnp.sum(jnp.where(eye, column, 0.0), axis=0, keepdims=True)

    own_ids = ids[group, 0:1].astype(f32)
    ids_column = jnp.sum(jnp.where(eye, own_ids, 0.0), axis=1, keepdims=True)
    user_low = cyc[group, 0]
    item_low = cyc[group, 1]

    def masks(g):
        diagonal = tile_columns + g * TOK == tile_rows + group * TOK
        same = ids[g, 0:1].astype(f32) == ids_column
        return diagonal, jnp.logical_and(same, jnp.logical_not(diagonal))

    def cycle_forward(g, carry):
        sums, own = carry
        logit = sharpen * dot(user_low, cyc[g, 1], 1, 1)
        diagonal, hidden = masks(g)
        value = jnp.where(hidden, 0.0, jnp.exp(logit))
        cexp[g] = value
        return sums + value, own + jnp.where(diagonal, logit, 0.0)

    zeros = jnp.zeros((TOK, TOK), f32)
    sums, own = lax.fori_loop(0, NG, cycle_forward, (zeros, zeros), unroll=2)
    cycle_total = jnp.sum(sums, axis=1, keepdims=True)
    own_logit = jnp.sum(own, axis=1, keepdims=True)

    z_step(gus, 1, zu_send, zu_recv)
    arrived(sel_in, ys_send, ys_recv, y_partner)
    sample_low = (select[:, :NEG] + sel_in[...].astype(f32)).astype(bf16)
    sample_exp = jnp.exp(sharpen * dot(user_low, sample_low))
    total = cycle_total + jnp.sum(sample_exp, axis=1, keepdims=True)
    total_row = to_row(total)
    tot_g[group] = jnp.broadcast_to(total_row, (8, TOK))
    tot_d[dev] = jnp.broadcast_to(total_row, (8, TOK))
    for k in range(1, ND):
        send(tot_d.at[dev], tot_d.at[dev], td_send.at[k - 1], td_recv.at[k - 1], dev_peers[k - 1])
    for k in range(1, NG):
        send(tot_g.at[group], tot_g.at[group], tg_send.at[k - 1], tg_recv.at[k - 1], group_peers[k - 1])
    loss_ref[...] = jnp.broadcast_to(to_row(jnp.log(total) - own_logit), (8, TOK))

    z_step(gus, 2, zu_send, zu_recv)
    inverse_total = 1.0 / total

    def user_backward(g, up):
        diagonal = tile_columns + g * TOK == tile_rows + group * TOK
        grad = ((cexp[g] * inverse_total - diagonal.astype(f32)) * factor).astype(bf16)
        return up + dot(grad, cyc[g, 1])

    sample_grad = (sample_exp * inverse_total * factor).astype(bf16)
    user_up = lax.fori_loop(0, NG, user_backward, dot(sample_grad, sample_low, 1, 1), unroll=2)
    user_back = unnormalize(unit_u[...], inv_u[...], user_up)
    grad_user_ref[...] = dot(uf[...], user_back, 0, 0)

    z_step(gus, 3, zu_send, zu_recv)
    for k in range(1, NG):
        arrived(tot_g.at[lax.rem(group + NG - k, NG)], tg_send.at[k - 1], tg_recv.at[k - 1], group_peers[k - 1])

    def item_backward(g, up):
        users = cyc[g, 0]
        diagonal, hidden = masks(g)
        value = jnp.where(hidden, 0.0, jnp.exp(sharpen * dot(item_low, users, 1, 1)))
        grad = ((value * (1.0 / tot_g[g, 0:1]) - diagonal.astype(f32)) * factor).astype(bf16)
        return up + dot(grad, users)

    item_up = lax.fori_loop(0, NG, item_backward, jnp.zeros((TOK, E), f32), unroll=2)
    item_back = unnormalize(unit_i[...], inv_i[...], item_up)
    z_step(gus, 4, zu_send, zu_recv)
    for k in range(1, ND):
        at = lax.rem(dev + ND - k, ND)
        arrived(codes.at[at], codes_send.at[k - 1], codes_recv.at[k - 1], dev_peers[k - 1])
        arrived(tot_d.at[at], td_send.at[k - 1], td_recv.at[k - 1], dev_peers[k - 1])
    owned[...] = jnp.zeros((OWN, E), f32)
    corpus_low = corp[z].reshape(OWN, E)
    code_rows = lax.broadcasted_iota(jnp.int32, (OWN, NEG), 0)
    ones = jnp.ones((NEG, 128), bf16)

    def corpus_backward(at, e):
        users = gus[at, e]
        holder = at * 2 + e
        value = jnp.exp(sharpen * dot(corpus_low, users, 1, 1))
        grad = (value * (1.0 / tot_d[holder, 0:1]) * factor).astype(bf16)
        back = unnormalize(unit_c[...], inv_c[...], dot(grad, users)).astype(f32)
        named = codes[holder]
        row = jnp.concatenate([named[n : n + 1] for n in range(4)], axis=1)
        hot = (row - dev * OWN == code_rows).astype(f32).astype(bf16)
        count = dot(hot, ones)
        owned[...] += jnp.concatenate([count, count], axis=1) * back

    def near_backward(i, carry):
        corpus_backward((z + NZ - 4 + i // 2) % NZ, i % 2)
        return carry

    lax.fori_loop(0, 18, near_backward, 0)
    for s in range(5, 9):
        z_step(gus, s, zu_send, zu_recv)

        def step_backward(i, carry, s=s):
            corpus_backward((z + NZ - s + (i // 2) * 2 * s) % NZ, i % 2)
            return carry

        lax.fori_loop(0, 4 if s < 8 else 2, step_backward, 0)
    high = owned[...].astype(bf16)
    low = (owned[...] - high.astype(f32)).astype(bf16)
    features = jnp.concatenate([itf[...], cf[...], cf[...]], axis=0)
    backs = jnp.concatenate([item_back, high, low], axis=0)
    grad_item_ref[...] = dot(features, backs, 0, 0)
    for copy in sends:
        copy.wait_send()


def local_grads(user_feat, item_feat, corpus_feat, user_weight, item_weight, ids, codes):
    dma, vmem = pltpu.SemaphoreType.DMA, pltpu.VMEM
    pairs = lambda *shape: [dma(shape), dma(shape)]
    return pl.pallas_call(
        local_grads_kernel,
        out_shape=[
            jax.ShapeDtypeStruct((8, TOK), f32),
            jax.ShapeDtypeStruct((WIDE, E), f32),
            jax.ShapeDtypeStruct((WIDE, E), f32),
        ],
        in_specs=[pl.BlockSpec(memory_space=pl.ANY)] * 7,
        out_specs=[pl.BlockSpec(memory_space=pltpu.VMEM)] * 3,
        scratch_shapes=[
            vmem((TOK, WIDE), bf16), vmem((TOK, WIDE), bf16), vmem((OWN, WIDE), bf16),
            vmem((WIDE, E), bf16), vmem((WIDE, E), bf16),
            vmem((NZ, 2, TOK, E), bf16), vmem((NZ, 2, TOK, E), bf16), vmem((NG, 2, TOK, E), bf16),
            vmem((NG, 8, 128), jnp.int32), vmem((ND, 8, 128), jnp.int32), vmem((8, 128), jnp.int32),
            vmem((NG, 8, 128), f32), vmem((ND, 8, 128), f32),
            vmem((E, 2 * NEG), f32), vmem((E, NEG), bf16), vmem((E, NEG), bf16), vmem((NG, TOK, TOK), f32),
            vmem((TOK, E), f32), vmem((TOK, E), f32), vmem((OWN, E), f32),
            vmem((TOK, 1), f32), vmem((TOK, 1), f32), vmem((OWN, 1), f32), vmem((OWN, E), f32),
            dma((7,)), *pairs(NG - 1), *pairs(ND - 1), *pairs(), *pairs(NG - 1), *pairs(ND - 1),
            *pairs(2, 8, 2), *pairs(2, 8, 2), *pairs(), *pairs(), *pairs(), *pairs(2, 3), *pairs(2, 4),
        ],
        compiler_params=pltpu.CompilerParams(
            collective_id=1, has_side_effects=True, vmem_limit_bytes=48 * 1024 * 1024
        ),
        name="local_grads",
    )(user_feat, item_feat, corpus_feat, user_weight, item_weight, ids, codes)


def local(
    user_feat, item_feat, item_ids, corpus_feat, neg_owner, neg_row, user_weight, item_weight
):
    ids = jnp.broadcast_to(item_ids[None, :], (8, TOK))
    code = neg_owner[:, 0] * OWN + neg_row
    codes = jnp.concatenate([code.reshape(4, 128)] * 2, axis=0)
    loss, grad_user, grad_item = local_grads(
        user_feat, item_feat, corpus_feat, user_weight, item_weight, ids, codes
    )
    grad_user, grad_item = reduce_all(grad_user, grad_item)
    return loss[0], grad_user, grad_item


def solution(mesh):
    return jax.shard_map(
        local,
        mesh=mesh,
        in_specs=(
            P(("group", "dev"), None),
            P(("group", "dev"), None),
            P(("group", "dev")),
            P(("group", "dev"), None),
            P(("group", "dev"), None),
            P(("group", "dev")),
            P(),
            P(),
        ),
        out_specs=(P(("group", "dev")), P(), P()),
        check_vma=False,
    )
```

```python
import jax
import jax.numpy as jnp
from jax import lax
from jax.experimental import pallas as pl
from jax.experimental.pallas import tpu as pltpu
from jax.sharding import PartitionSpec as P

sharpen = 20.0
epsilon = 1e-06
MESH = pl.DeviceIdType.MESH
NX, NY, NZ = 4, 4, 16


def place():
    group, dev = lax.axis_index("group"), lax.axis_index("dev")
    core, x, y_hi = group % 2, (group // 2) % NX, group // (2 * NX)
    z, y_lo = dev // 2, dev % 2
    return core, x, y_hi * 2 + y_lo, z


def device_at(core, x, y, z):
    return (((y // 2) * NX + x) * 2 + core, z * 2 + y % 2)


def greet(partners):
    barrier = pltpu.get_barrier_semaphore()
    for partner in partners:
        pl.semaphore_signal(barrier, inc=1, device_id=partner, device_id_type=MESH)
    pl.semaphore_wait(barrier, len(partners))


def remote(src, dst, send_sem, recv_sem, device):
    return pltpu.make_async_remote_copy(
        src_ref=src, dst_ref=dst, send_sem=send_sem, recv_sem=recv_sem, device_id=device, device_id_type=MESH
    )


TOK, OWN, NEG, WIDE, E = 128, 256, 512, 1024, 256
NG, ND = 16, 32
f32, bf16 = jnp.float32, jnp.bfloat16


def dot(left, right, left_dim=1, right_dim=0):
    return lax.dot_general(left, right, (((left_dim,), (right_dim,)), ((), ())), preferred_element_type=f32)


def project(features, weight):
    hidden = dot(features, weight)
    inverse = lax.rsqrt(jnp.sum(hidden * hidden, axis=-1, keepdims=True) + epsilon)
    return hidden * inverse, inverse


def unnormalize(unit, inverse, upstream):
    along = jnp.sum(unit * upstream, axis=-1, keepdims=True)
    return ((upstream - unit * along) * inverse).astype(bf16)


FOLD = 512
PART = 128
BIT = 32


def step_kernel(
    user_feat, item_feat, corpus_feat, user_weight, item_weight, ids_in, owner_in, row_in,
    loss_ref, out_ref,
    uf, itf, cf, uw, iw, ids_own, owner_own, row_own, corp, gus, cyc, ids, codes, pair_codes, tot_g, tot_d,
    select, sel_out, sel_in, cexp, sums, own_sums, unit_u, unit_i, unit_c, inv_u, inv_i, inv_c, upward, owned,
    mine, from_core, from_first, from_second, from_z,
    load_sem, ids_send, ids_recv, codes_send, codes_recv, pair_send, pair_recv, tg_send, tg_recv, td_send, td_recv,
    zc_send, zc_recv, zu_send, zu_recv, yu_send, yu_recv, ys_send, ys_recv,
    yh_send, yh_recv, x_send, x_recv, c_send, c_recv,
    core_send, core_recv, first_send, first_recv, second_send, second_recv, z_sends, z_recvs,
    zg_send, zg_recv, sg_send, sg_recv, fg_send, fg_recv, cg_send, cg_recv,
):
    core, x, y, z = place()
    y_hi, y_lo = y // 2, y % 2
    group, dev = lax.axis_index("group"), lax.axis_index("dev")
    factor = sharpen / TOK
    loads = [
        pltpu.make_async_copy(src, dst, load_sem.at[n])
        for n, (src, dst) in enumerate([
            (corpus_feat, cf), (item_weight, iw), (user_feat, uf), (user_weight, uw), (item_feat, itf),
            (ids_in, ids_own), (owner_in, owner_own), (row_in, row_own),
        ])
    ]
    for load in loads:
        load.start()
    group_peers = [(lax.rem(group + k, NG), dev) for k in range(1, NG)]
    dev_peers = [(group, lax.rem(dev + k, ND)) for k in range(1, ND)]
    sibling = device_at(1 - core, x, y, z)
    y_partner = device_at(core, x, y_hi * 2 + 1 - y_lo, z)
    y_far = device_at(core, x, (1 - y_hi) * 2 + y_lo, z)
    x_peers = [device_at(core, (x + k) % NX, y, z) for k in range(1, NX)]
    y_peers = [device_at(core, x, (y + k) % NY, z) for k in range(1, NY)]
    z_all = [device_at(core, x, y, (z + k) % NZ) for k in range(1, NZ)]
    z_peers = [z_all[0], z_all[-1]]
    sends = []

    def send(src, dst, send_sem, recv_sem, device):
        copy = remote(src, dst, send_sem, recv_sem, device)
        copy.start()
        sends.append(copy)

    def arrived(dst, send_sem, recv_sem, device):
        remote(dst, dst, send_sem, recv_sem, device).wait_recv()

    barrier = pltpu.get_barrier_semaphore()
    greeted = group_peers + dev_peers + [device_at(core, x, NY - 1 - y, z)]
    for partner in greeted:
        pl.semaphore_signal(barrier, inc=1, device_id=partner, device_id_type=MESH)

    first_at, second_at = [x, y], [y, x]
    along = [x_peers, y_peers]

    def part_rows(fold, part):
        return pl.ds(pl.multiple_of(fold * FOLD + part * PART, PART), PART)

    def bit_rows(fold, part, bit):
        return pl.ds(pl.multiple_of(fold * FOLD + part * PART + bit * BIT, BIT), BIT)

    def tile_of(at):
        fold = at // 8
        row = fold * FOLD + (x + fold * (y - x)) * PART + (y + fold * (x - y)) * BIT + ((at // 2) % 4) * 8
        return pl.ds(pl.multiple_of(row, 8), 8), pl.ds(pl.multiple_of((at % 2) * 128, 128), 128)

    order = [(k, fold) for k in (1, 2, 3, 0) for fold in (0, 1)]
    far_order = [(k, fold) for k in (1, 2, 3) for fold in (0, 1)]

    def order_rows(n):
        k, fold = order[n]
        return part_rows(fold, (first_at[fold] + k) % 4)

    def core_copy(q, n):
        return remote(mine.at[q, order_rows(n)], from_core.at[n], core_send.at[n], core_recv.at[n], sibling)

    def first_copy(q, k, fold):
        rows = part_rows(fold, (first_at[fold] + k) % 4)
        return remote(
            mine.at[q, rows], from_first.at[fold, k - 1], first_send.at[fold, k - 1], first_recv.at[fold, k - 1],
            along[fold][k - 1],
        )

    def second_copy(q, k, fold):
        rows = bit_rows(fold, first_at[fold], (second_at[fold] + k) % 4)
        return remote(
            mine.at[q, rows], from_second.at[fold, k - 1], second_send.at[fold, k - 1], second_recv.at[fold, k - 1],
            along[1 - fold][k - 1],
        )

    def z_copy(q, k):
        rows, columns = tile_of((z + k) % NZ)
        return remote(mine.at[q, rows, columns], from_z.at[k - 1], z_sends.at[k - 1], z_recvs.at[k - 1], z_all[k - 1])

    def zg_copy(q, k, back):
        rows, columns = tile_of((z + NZ - k * back) % NZ)
        tile = out_ref.at[q, rows, columns]
        return remote(tile, tile, zg_send.at[k - 1], zg_recv.at[k - 1], z_all[k - 1])

    def sg_copy(q, k, fold, back):
        bit = out_ref.at[q, bit_rows(fold, first_at[fold], (second_at[fold] + 4 - k * back) % 4)]
        return remote(bit, bit, sg_send.at[fold, k - 1], sg_recv.at[fold, k - 1], along[1 - fold][k - 1])

    def fg_copy(q, k, fold, back):
        part = out_ref.at[q, part_rows(fold, (first_at[fold] + 4 - k * back) % 4)]
        return remote(part, part, fg_send.at[fold, k - 1], fg_recv.at[fold, k - 1], along[fold][k - 1])

    def cg_copy(q, k, fold):
        part = out_ref.at[q, part_rows(fold, (first_at[fold] + 4 - k) % 4)]
        return remote(part, part, cg_send.at[fold, k], cg_recv.at[fold, k], sibling)

    def reduce_first(q):
        for n, (k, fold) in enumerate(order):
            rows = order_rows(n)
            core_copy(q, n).wait_recv()
            mine[q, rows] += from_core[n]
            if k:
                first_copy(q, k, fold).start()

    def reduce_second(q):
        for k, fold in far_order:
            first_copy(q, k, fold).wait_recv()
        for k, fold in order:
            at = (second_at[fold] + k) % 4
            rows = bit_rows(fold, first_at[fold], at)
            near = pl.ds(pl.multiple_of(at * BIT, BIT), BIT)
            mine[q, rows] += from_first[fold, 0, near] + from_first[fold, 1, near] + from_first[fold, 2, near]
            if k:
                second_copy(q, k, fold).start()

    def reduce_z(q):
        for k, fold in far_order:
            second_copy(q, k, fold).wait_recv()
        for fold in (0, 1):
            rows = bit_rows(fold, first_at[fold], second_at[fold])
            mine[q, rows] += from_second[fold, 0] + from_second[fold, 1] + from_second[fold, 2]
        for k in range(1, NZ):
            z_copy(q, k).start()

    def gather_z(q):
        rows, columns = tile_of(z)
        total = mine[q, rows, columns]
        for k in range(1, NZ):
            z_copy(q, k).wait_recv()
            total = total + from_z[k - 1]
        out_ref[q, rows, columns] = total
        for k in range(1, NZ):
            zg_copy(q, k, 0).start()

    def gather_rest(q):
        for k in range(1, NZ):
            zg_copy(q, k, 1).wait_recv()
        for k, fold in far_order:
            sg_copy(q, k, fold, 0).start()
        for k, fold in far_order:
            sg_copy(q, k, fold, 1).wait_recv()
        for k, fold in far_order:
            fg_copy(q, k, fold, 0).start()
        for fold in (0, 1):
            cg_copy(q, 0, fold).start()
        for k, fold in far_order:
            fg_copy(q, k, fold, 1).wait_recv()
            cg_copy(q, k, fold).start()
        for k, fold in far_order:
            first_copy(q, k, fold).wait_send()
            second_copy(q, k, fold).wait_send()
            sg_copy(q, k, fold, 0).wait_send()
            fg_copy(q, k, fold, 0).wait_send()
        for k in range(1, NZ):
            z_copy(q, k).wait_send()
            zg_copy(q, k, 0).wait_send()
        for k, fold in order:
            cg_copy(q, k, fold).wait_send()

    def take_gathered(q):
        for k, fold in order:
            cg_copy(q, k, fold).wait_recv()
        for n in range(len(order)):
            core_copy(q, n).wait_send()

    def on_core(which, action, *given):
        @pl.when(core == which)
        def _():
            action(*given)

    loads[0].wait()
    loads[1].wait()
    unit, inverse = project(cf[...], iw[...])
    unit_c[...] = unit
    inv_c[...] = inverse
    corp[z] = unit.astype(bf16).reshape(2, TOK, E)
    pl.semaphore_wait(barrier, len(greeted))

    def z_send(buf, at, s, e, way, send_sem, recv_sem):
        send(buf.at[at, e], buf.at[at, e], send_sem.at[way, s - 1, e], recv_sem.at[way, s - 1, e], z_peers[way])

    def source(way, s):
        return (z + NZ - s) % NZ if way == 0 else (z + s) % NZ

    def z_step(buf, s, send_sem, recv_sem, work=()):
        work = list(work)
        for e in (0, 1):
            for way in (0, 1):
                if s == 8 and e != way:
                    continue
                at = source(way, s)
                arrived(buf.at[at, e], send_sem.at[way, s - 1, e], recv_sem.at[way, s - 1, e], z_peers[way])
                if s < 7 or (s == 7 and e == way):
                    z_send(buf, at, s + 1, e, way, send_sem, recv_sem)
                if work:
                    work.pop(0)()
        for piece in work:
            piece()

    for e in (0, 1):
        for way in (0, 1):
            z_send(corp, z, 1, e, way, zc_send, zc_recv)
    for load in loads[5:]:
        load.wait()
    code = owner_own[...] * OWN + row_own[...]
    codes[dev] = jnp.concatenate([code, code], axis=0)
    ids[group] = jnp.broadcast_to(ids_own[...], (8, TOK))
    send(codes.at[dev], pair_codes, pair_send, pair_recv, y_partner)

    loads[2].wait()
    loads[3].wait()
    unit, inverse = project(uf[...], uw[...])
    unit_u[...] = unit
    inv_u[...] = inverse
    user_low = unit.astype(bf16)
    cyc[group, 0] = user_low
    gus[z, y_lo] = user_low
    loads[4].wait()
    unit, inverse = project(itf[...], iw[...])
    unit_i[...] = unit
    inv_i[...] = inverse
    item_low = unit.astype(bf16)
    cyc[group, 1] = item_low
    far_group = lax.rem(group + NG // 2, NG)
    send(cyc.at[group], cyc.at[group], yh_send, yh_recv, y_far)
    for k in range(1, NX):
        send(cyc.at[group], cyc.at[group], x_send.at[0, k - 1], x_recv.at[0, k - 1], x_peers[k - 1])
    send(gus.at[z, y_lo], gus.at[z, y_lo], yu_send, yu_recv, y_partner)
    send(cyc.at[group], cyc.at[group], c_send.at[0, 0], c_recv.at[0, 0], sibling)

    def group_of(far, k, other):
        row = y_hi + far * (1 - 2 * y_hi)
        return (row * NX + (x + NX - k) % NX) * 2 + core + other * (1 - 2 * core)

    arrived(pair_codes, pair_send, pair_recv, y_partner)
    own_codes, their_codes = codes[dev], pair_codes[...]
    code_row = jnp.concatenate(
        [own_codes[n : n + 1] for n in range(4)] + [their_codes[n : n + 1] for n in range(4)], axis=1
    )
    wide_rows = lax.broadcasted_iota(jnp.int32, (OWN, 2 * NEG), 0)

    def select_from(at):
        hot = (code_row - (at * 2 + y_lo) * OWN == wide_rows).astype(f32).astype(bf16)
        return dot(corp[at].reshape(OWN, E), hot, 0, 0)

    def nothing():
        pass

    def select_more(way, s):
        def piece():
            select[...] += select_from(source(way, s))

        return piece

    select[...] = select_from(z)
    for s in range(1, 9):
        work = [nothing, select_more(0, s - 1), nothing, select_more(1, s - 1)] if s > 1 else []
        z_step(corp, s, zc_send, zc_recv, work)
        if s == 1:
            for k in range(1, ND):
                send(codes.at[dev], codes.at[dev], codes_send.at[k - 1], codes_recv.at[k - 1], dev_peers[k - 1])
        if s == 2:
            arrived(cyc.at[far_group], yh_send, yh_recv, y_far)
            for k in range(1, NX):
                send(cyc.at[far_group], cyc.at[far_group], x_send.at[1, k - 1], x_recv.at[1, k - 1], x_peers[k - 1])
            send(cyc.at[far_group], cyc.at[far_group], c_send.at[1, 0], c_recv.at[1, 0], sibling)
        if s == 3:
            for k in range(1, NG):
                send(ids.at[group], ids.at[group], ids_send.at[k - 1], ids_recv.at[k - 1], group_peers[k - 1])
        if s in (4, 6):
            far = (s - 4) // 2
            for k in range(1, NX):
                block = cyc.at[group_of(far, k, 0)]
                arrived(block, x_send.at[far, k - 1], x_recv.at[far, k - 1], x_peers[k - 1])
                send(block, block, c_send.at[far, k], c_recv.at[far, k], sibling)
        if s == 7:
            arrived(gus.at[z, 1 - y_lo], yu_send, yu_recv, y_partner)
            for e in (0, 1):
                for way in (0, 1):
                    z_send(gus, z, 1, e, way, zu_send, zu_recv)
    select[...] += select_from(source(0, 8))
    sel_out[...] = select[:, NEG:].astype(bf16)
    send(sel_out, sel_in, ys_send, ys_recv, y_partner)

    for far in (0, 1):
        for k in range(NX):
            arrived(cyc.at[group_of(far, k, 1)], c_send.at[far, k], c_recv.at[far, k], sibling)
    for k in range(1, NG):
        arrived(ids.at[lax.rem(group + NG - k, NG)], ids_send.at[k - 1], ids_recv.at[k - 1], group_peers[k - 1])

    tile_rows = lax.broadcasted_iota(jnp.int32, (TOK, TOK), 0)
    tile_columns = lax.broadcasted_iota(jnp.int32, (TOK, TOK), 1)
    eye = tile_rows == tile_columns

    def to_row(column):
        return jnp.sum(jnp.where(eye, column, 0.0), axis=0, keepdims=True)

    own_ids = ids_own[...].astype(f32)
    ids_column = jnp.sum(jnp.where(eye, own_ids, 0.0), axis=1, keepdims=True)
    user_low = cyc[group, 0]
    item_low = cyc[group, 1]

    def masks(g):
        diagonal = tile_columns + g * TOK == tile_rows + group * TOK
        same = ids[g, 0:1].astype(f32) == ids_column
        return diagonal, jnp.logical_and(same, jnp.logical_not(diagonal))

    def cycle_forward(g, carry):
        logit = sharpen * dot(user_low, cyc[g, 1], 1, 1)
        diagonal, hidden = masks(g)
        value = jnp.where(hidden, 0.0, jnp.exp(logit))
        cexp[g] = value
        return carry[0] + value, carry[1] + jnp.where(diagonal, logit, 0.0)

    def forward_piece(n):
        def piece():
            sums[...], own_sums[...] = lax.fori_loop(
                4 * n, 4 * n + 4, cycle_forward, (sums[...], own_sums[...]), unroll=2
            )

        return piece

    sums[...] = jnp.zeros((TOK, TOK), f32)
    own_sums[...] = jnp.zeros((TOK, TOK), f32)
    z_step(gus, 1, zu_send, zu_recv, [forward_piece(n) for n in range(4)])
    arrived(sel_in, ys_send, ys_recv, y_partner)
    sample_low = (select[:, :NEG] + sel_in[...].astype(f32)).astype(bf16)
    sample_exp = jnp.exp(sharpen * dot(user_low, sample_low))
    total = jnp.sum(sums[...], axis=1, keepdims=True) + jnp.sum(sample_exp, axis=1, keepdims=True)
    total_row = to_row(total)
    tot_g[group] = jnp.broadcast_to(total_row, (8, TOK))
    tot_d[dev] = jnp.broadcast_to(total_row, (8, TOK))
    for k in range(1, ND):
        send(tot_d.at[dev], tot_d.at[dev], td_send.at[k - 1], td_recv.at[k - 1], dev_peers[k - 1])
    for k in range(1, NG):
        send(tot_g.at[group], tot_g.at[group], tg_send.at[k - 1], tg_recv.at[k - 1], group_peers[k - 1])
    own_logit = jnp.sum(own_sums[...], axis=1, keepdims=True)
    loss_ref[...] = jnp.broadcast_to(to_row(jnp.log(total) - own_logit), (8, TOK))
    inverse_total = 1.0 / total
    sample_grad = (sample_exp * inverse_total * factor).astype(bf16)

    def user_backward(g, up):
        diagonal = tile_columns + g * TOK == tile_rows + group * TOK
        grad = ((cexp[g] * inverse_total - diagonal.astype(f32)) * factor).astype(bf16)
        return up + dot(grad, cyc[g, 1])

    def user_piece(n):
        def piece():
            start = upward[...] if n else dot(sample_grad, sample_low, 1, 1)
            upward[...] = lax.fori_loop(4 * n, 4 * n + 4, user_backward, start, unroll=2)

        return piece

    z_step(gus, 2, zu_send, zu_recv, [user_piece(n) for n in range(4)])
    user_back = unnormalize(unit_u[...], inv_u[...], upward[...])

    def user_part(n):
        rows = order_rows(n)
        mine[0, rows] = dot(uf[:, rows], user_back, 0, 0)
        on_core(1, lambda: core_copy(0, n).start())

    def user_parts(n):
        def piece():
            user_part(2 * n)
            user_part(2 * n + 1)

        return piece

    z_step(gus, 3, zu_send, zu_recv, [user_parts(n) for n in range(4)])
    for k in range(1, NG):
        arrived(tot_g.at[lax.rem(group + NG - k, NG)], tg_send.at[k - 1], tg_recv.at[k - 1], group_peers[k - 1])

    def item_backward(g, up):
        users = cyc[g, 0]
        diagonal, hidden = masks(g)
        value = jnp.where(hidden, 0.0, jnp.exp(sharpen * dot(item_low, users, 1, 1)))
        grad = ((value * (1.0 / tot_g[g, 0:1]) - diagonal.astype(f32)) * factor).astype(bf16)
        return up + dot(grad, users)

    def item_piece(n):
        def piece():
            start = upward[...] if n else jnp.zeros((TOK, E), f32)
            upward[...] = lax.fori_loop(4 * n, 4 * n + 4, item_backward, start, unroll=2)

        return piece

    z_step(gus, 4, zu_send, zu_recv, [item_piece(n) for n in range(4)])
    item_back = unnormalize(unit_i[...], inv_i[...], upward[...])
    mine[1] = dot(itf[...], item_back, 0, 0)
    on_core(0, reduce_first, 0)
    for k in range(1, ND):
        at = lax.rem(dev + ND - k, ND)
        arrived(codes.at[at], codes_send.at[k - 1], codes_recv.at[k - 1], dev_peers[k - 1])
        arrived(tot_d.at[at], td_send.at[k - 1], td_recv.at[k - 1], dev_peers[k - 1])
    owned[...] = jnp.zeros((OWN, E), f32)
    corpus_low = corp[z].reshape(OWN, E)
    code_rows = lax.broadcasted_iota(jnp.int32, (OWN, NEG), 0)
    ones = jnp.ones((NEG, 128), bf16)

    def corpus_backward(j, carry):
        s = (j + 2) // 4
        at = (z + NZ - s + 2 * s * (((j + 2) % 4) // 2)) % NZ
        e = j % 2
        users = gus[at, e]
        holder = at * 2 + e
        value = jnp.exp(sharpen * dot(corpus_low, users, 1, 1))
        grad = (value * (1.0 / tot_d[holder, 0:1]) * factor).astype(bf16)
        back = unnormalize(unit_c[...], inv_c[...], dot(grad, users)).astype(f32)
        named = codes[holder]
        row = jnp.concatenate([named[n : n + 1] for n in range(4)], axis=1)
        hot = (row - dev * OWN == code_rows).astype(f32).astype(bf16)
        count = dot(hot, ones)
        owned[...] += jnp.concatenate([count, count], axis=1) * back
        return carry

    def corpus_piece(first, last):
        return lambda: lax.fori_loop(first, last, corpus_backward, 0)

    z_step(gus, 5, zu_send, zu_recv, [corpus_piece(3 * n, 3 * n + 3) for n in range(4)])
    on_core(0, reduce_second, 0)
    z_step(gus, 6, zu_send, zu_recv, [corpus_piece(12 + 2 * n, 14 + 2 * n) for n in range(4)])
    on_core(0, reduce_z, 0)
    z_step(gus, 7, zu_send, zu_recv, [corpus_piece(20, 22), corpus_piece(22, 24), corpus_piece(24, 26)])
    z_step(gus, 8, zu_send, zu_recv, [corpus_piece(26, 28), corpus_piece(28, 30)])
    corpus_piece(30, 32)()
    high = owned[...].astype(bf16)
    low = (owned[...] - high.astype(f32)).astype(bf16)
    for n in range(len(order)):
        rows = order_rows(n)
        mine[1, rows] += dot(cf[:, rows], high, 0, 0) + dot(cf[:, rows], low, 0, 0)
        on_core(0, lambda: core_copy(1, n).start())
    on_core(1, reduce_first, 1)
    on_core(1, reduce_second, 1)
    on_core(1, reduce_z, 1)
    on_core(1, gather_z, 1)
    on_core(1, gather_rest, 1)
    on_core(0, gather_z, 0)
    on_core(0, gather_rest, 0)
    on_core(1, take_gathered, 0)
    on_core(0, take_gathered, 1)
    for copy in sends:
        copy.wait_send()


def step(user_feat, item_feat, corpus_feat, user_weight, item_weight, ids, owners, rows):
    dma, vmem = pltpu.SemaphoreType.DMA, pltpu.VMEM
    pairs = lambda *shape: [dma(shape), dma(shape)]
    return pl.pallas_call(
        step_kernel,
        out_shape=[jax.ShapeDtypeStruct((8, TOK), f32), jax.ShapeDtypeStruct((2, WIDE, E), f32)],
        in_specs=[pl.BlockSpec(memory_space=pl.ANY)] * 8,
        out_specs=[pl.BlockSpec(memory_space=pltpu.VMEM)] * 2,
        scratch_shapes=[
            vmem((TOK, WIDE), bf16), vmem((TOK, WIDE), bf16), vmem((OWN, WIDE), bf16),
            vmem((WIDE, E), bf16), vmem((WIDE, E), bf16),
            vmem((1, TOK), jnp.int32), vmem((4, 128), jnp.int32), vmem((4, 128), jnp.int32),
            vmem((NZ, 2, TOK, E), bf16), vmem((NZ, 2, TOK, E), bf16), vmem((NG, 2, TOK, E), bf16),
            vmem((NG, 8, 128), jnp.int32), vmem((ND, 8, 128), jnp.int32), vmem((8, 128), jnp.int32),
            vmem((NG, 8, 128), f32), vmem((ND, 8, 128), f32),
            vmem((E, 2 * NEG), f32), vmem((E, NEG), bf16), vmem((E, NEG), bf16), vmem((NG, TOK, TOK), f32),
            vmem((TOK, TOK), f32), vmem((TOK, TOK), f32),
            vmem((TOK, E), f32), vmem((TOK, E), f32), vmem((OWN, E), f32),
            vmem((TOK, 1), f32), vmem((TOK, 1), f32), vmem((OWN, 1), f32), vmem((TOK, E), f32), vmem((OWN, E), f32),
            vmem((2, WIDE, E), f32), vmem((8, PART, E), f32), vmem((2, 3, PART, E), f32), vmem((2, 3, BIT, E), f32),
            vmem((NZ - 1, 8, 128), f32),
            dma((8,)), *pairs(NG - 1), *pairs(ND - 1), *pairs(), *pairs(NG - 1), *pairs(ND - 1),
            *pairs(2, 8, 2), *pairs(2, 8, 2), *pairs(), *pairs(), *pairs(), *pairs(2, 3), *pairs(2, 4),
            *pairs(8), *pairs(2, 3), *pairs(2, 3), *pairs(NZ - 1), *pairs(NZ - 1), *pairs(2, 3), *pairs(2, 3),
            *pairs(2, 4),
        ],
        compiler_params=pltpu.CompilerParams(
            collective_id=0, has_side_effects=True, vmem_limit_bytes=60 * 1024 * 1024
        ),
        name="step",
    )(user_feat, item_feat, corpus_feat, user_weight, item_weight, ids, owners, rows)


def local(
    user_feat, item_feat, item_ids, corpus_feat, neg_owner, neg_row, user_weight, item_weight
):
    loss, grads = step(
        user_feat, item_feat, corpus_feat, user_weight, item_weight,
        item_ids.reshape(1, TOK), neg_owner.reshape(4, 128), neg_row.reshape(4, 128),
    )
    return loss[0], grads[0], grads[1]


def solution(mesh):
    return jax.shard_map(
        local,
        mesh=mesh,
        in_specs=(
            P(("group", "dev"), None),
            P(("group", "dev"), None),
            P(("group", "dev")),
            P(("group", "dev"), None),
            P(("group", "dev"), None),
            P(("group", "dev")),
            P(),
            P(),
        ),
        out_specs=(P(("group", "dev")), P(), P()),
        check_vma=False,
    )
```

```python
import jax
import jax.numpy as jnp
from jax import lax
from jax.experimental import pallas as pl
from jax.experimental.pallas import tpu as pltpu
from jax.sharding import PartitionSpec as P

sharpen = 20.0
epsilon = 1e-06
MESH = pl.DeviceIdType.MESH
NX, NY, NZ = 4, 4, 16


def place():
    group, dev = lax.axis_index("group"), lax.axis_index("dev")
    core, x, y_hi = group % 2, (group // 2) % NX, group // (2 * NX)
    z, y_lo = dev // 2, dev % 2
    return core, x, y_hi * 2 + y_lo, z


def device_at(core, x, y, z):
    return (((y // 2) * NX + x) * 2 + core, z * 2 + y % 2)


def greet(partners):
    barrier = pltpu.get_barrier_semaphore()
    for partner in partners:
        pl.semaphore_signal(barrier, inc=1, device_id=partner, device_id_type=MESH)
    pl.semaphore_wait(barrier, len(partners))


def remote(src, dst, send_sem, recv_sem, device):
    return pltpu.make_async_remote_copy(
        src_ref=src, dst_ref=dst, send_sem=send_sem, recv_sem=recv_sem, device_id=device, device_id_type=MESH
    )


TOK, OWN, NEG, WIDE, E = 128, 256, 512, 1024, 256
NG, ND = 16, 32
QUAD = 4
f32, bf16 = jnp.float32, jnp.bfloat16


def dot(left, right, left_dim=1, right_dim=0):
    return lax.dot_general(left, right, (((left_dim,), (right_dim,)), ((), ())), preferred_element_type=f32)


def project(features, weight):
    hidden = dot(features, weight)
    inverse = lax.rsqrt(jnp.sum(hidden * hidden, axis=-1, keepdims=True) + epsilon)
    return hidden * inverse, inverse


def unnormalize(unit, inverse, upstream):
    along = jnp.sum(unit * upstream, axis=-1, keepdims=True)
    return ((upstream - unit * along) * inverse).astype(bf16)


FOLD = 512
PART = 128
BIT = 32


def step_kernel(
    user_feat, item_feat, corpus_feat, user_weight, item_weight, ids_in, owner_in, row_in,
    loss_ref, out_ref,
    uf, itf, cf, uw, iw, ids_own, owner_own, row_own, corp, gus, cyc, ids, codes, pair_codes, tot_g, tot_d,
    select, sel_out, sel_in, cexp, counts, sums, own_sums, unit_u, unit_i, unit_c, inv_u, inv_i, inv_c, upward, owned,
    mine, from_core, from_first, from_second, from_z,
    load_sem, ids_send, ids_recv, codes_send, codes_recv, pair_send, pair_recv, tg_send, tg_recv, td_send, td_recv,
    zc_send, zc_recv, zu_send, zu_recv, yu_send, yu_recv, ys_send, ys_recv,
    yh_send, yh_recv, x_send, x_recv, c_send, c_recv,
    core_send, core_recv, first_send, first_recv, second_send, second_recv, z_sends, z_recvs,
    zg_send, zg_recv, sg_send, sg_recv, fg_send, fg_recv, cg_send, cg_recv,
):
    core, x, y, z = place()
    y_hi, y_lo = y // 2, y % 2
    group, dev = lax.axis_index("group"), lax.axis_index("dev")
    factor = sharpen / TOK
    loads = [
        pltpu.make_async_copy(src, dst, load_sem.at[n])
        for n, (src, dst) in enumerate([
            (corpus_feat, cf), (item_weight, iw), (user_feat, uf), (user_weight, uw), (item_feat, itf),
            (ids_in, ids_own), (owner_in, owner_own), (row_in, row_own),
        ])
    ]
    for load in loads:
        load.start()
    group_peers = [(lax.rem(group + k, NG), dev) for k in range(1, NG)]
    dev_peers = [(group, lax.rem(dev + k, ND)) for k in range(1, ND)]
    sibling = device_at(1 - core, x, y, z)
    y_partner = device_at(core, x, y_hi * 2 + 1 - y_lo, z)
    y_far = device_at(core, x, (1 - y_hi) * 2 + y_lo, z)
    x_peers = [device_at(core, (x + k) % NX, y, z) for k in range(1, NX)]
    y_peers = [device_at(core, x, (y + k) % NY, z) for k in range(1, NY)]
    z_all = [device_at(core, x, y, (z + k) % NZ) for k in range(1, NZ)]
    z_peers = [z_all[0], z_all[-1]]
    sends = []

    def send(src, dst, send_sem, recv_sem, device):
        copy = remote(src, dst, send_sem, recv_sem, device)
        copy.start()
        sends.append(copy)

    def arrived(dst, send_sem, recv_sem, device):
        remote(dst, dst, send_sem, recv_sem, device).wait_recv()

    barrier = pltpu.get_barrier_semaphore()
    greeted = group_peers + dev_peers + [device_at(core, x, NY - 1 - y, z)]
    for partner in greeted:
        pl.semaphore_signal(barrier, inc=1, device_id=partner, device_id_type=MESH)

    first_at, second_at = [x, y], [y, x]
    along = [x_peers, y_peers]

    def part_rows(fold, part):
        return pl.ds(pl.multiple_of(fold * FOLD + part * PART, PART), PART)

    def bit_rows(fold, part, bit):
        return pl.ds(pl.multiple_of(fold * FOLD + part * PART + bit * BIT, BIT), BIT)

    def tile_of(at):
        fold = at // 8
        row = fold * FOLD + (x + fold * (y - x)) * PART + (y + fold * (x - y)) * BIT + ((at // 2) % 4) * 8
        return pl.ds(pl.multiple_of(row, 8), 8), pl.ds(pl.multiple_of((at % 2) * 128, 128), 128)

    order = [(k, fold) for k in (1, 2, 3, 0) for fold in (0, 1)]
    far_order = [(k, fold) for k in (1, 2, 3) for fold in (0, 1)]

    def order_rows(n):
        k, fold = order[n]
        return part_rows(fold, (first_at[fold] + k) % 4)

    def core_copy(q, n):
        return remote(mine.at[q, order_rows(n)], from_core.at[n], core_send.at[n], core_recv.at[n], sibling)

    def first_copy(q, k, fold):
        rows = part_rows(fold, (first_at[fold] + k) % 4)
        return remote(
            mine.at[q, rows], from_first.at[fold, k - 1], first_send.at[fold, k - 1], first_recv.at[fold, k - 1],
            along[fold][k - 1],
        )

    def second_copy(q, k, fold):
        rows = bit_rows(fold, first_at[fold], (second_at[fold] + k) % 4)
        return remote(
            mine.at[q, rows], from_second.at[fold, k - 1], second_send.at[fold, k - 1], second_recv.at[fold, k - 1],
            along[1 - fold][k - 1],
        )

    def z_copy(q, k):
        rows, columns = tile_of((z + k) % NZ)
        return remote(mine.at[q, rows, columns], from_z.at[k - 1], z_sends.at[k - 1], z_recvs.at[k - 1], z_all[k - 1])

    def zg_copy(q, k, back):
        rows, columns = tile_of((z + NZ - k * back) % NZ)
        tile = out_ref.at[q, rows, columns]
        return remote(tile, tile, zg_send.at[k - 1], zg_recv.at[k - 1], z_all[k - 1])

    def sg_copy(q, k, fold, back):
        bit = out_ref.at[q, bit_rows(fold, first_at[fold], (second_at[fold] + 4 - k * back) % 4)]
        return remote(bit, bit, sg_send.at[fold, k - 1], sg_recv.at[fold, k - 1], along[1 - fold][k - 1])

    def fg_copy(q, k, fold, back):
        part = out_ref.at[q, part_rows(fold, (first_at[fold] + 4 - k * back) % 4)]
        return remote(part, part, fg_send.at[fold, k - 1], fg_recv.at[fold, k - 1], along[fold][k - 1])

    def cg_copy(q, k, fold):
        part = out_ref.at[q, part_rows(fold, (first_at[fold] + 4 - k) % 4)]
        return remote(part, part, cg_send.at[fold, k], cg_recv.at[fold, k], sibling)

    def reduce_first(q):
        for n, (k, fold) in enumerate(order):
            rows = order_rows(n)
            core_copy(q, n).wait_recv()
            mine[q, rows] += from_core[n]
            if k:
                first_copy(q, k, fold).start()

    def reduce_second(q):
        for k, fold in far_order:
            first_copy(q, k, fold).wait_recv()
        for k, fold in order:
            at = (second_at[fold] + k) % 4
            rows = bit_rows(fold, first_at[fold], at)
            near = pl.ds(pl.multiple_of(at * BIT, BIT), BIT)
            mine[q, rows] += from_first[fold, 0, near] + from_first[fold, 1, near] + from_first[fold, 2, near]
            if k:
                second_copy(q, k, fold).start()

    def reduce_z(q):
        for k, fold in far_order:
            second_copy(q, k, fold).wait_recv()
        for fold in (0, 1):
            rows = bit_rows(fold, first_at[fold], second_at[fold])
            mine[q, rows] += from_second[fold, 0] + from_second[fold, 1] + from_second[fold, 2]
        for k in range(1, NZ):
            z_copy(q, k).start()

    def gather_z(q):
        rows, columns = tile_of(z)
        total = mine[q, rows, columns]
        for k in range(1, NZ):
            z_copy(q, k).wait_recv()
            total = total + from_z[k - 1]
        out_ref[q, rows, columns] = total
        for k in range(1, NZ):
            zg_copy(q, k, 0).start()

    def gather_rest(q):
        for k in range(1, NZ):
            zg_copy(q, k, 1).wait_recv()
        for k, fold in far_order:
            sg_copy(q, k, fold, 0).start()
        for k, fold in far_order:
            sg_copy(q, k, fold, 1).wait_recv()
        for k, fold in far_order:
            fg_copy(q, k, fold, 0).start()
        for fold in (0, 1):
            cg_copy(q, 0, fold).start()
        for k, fold in far_order:
            fg_copy(q, k, fold, 1).wait_recv()
            cg_copy(q, k, fold).start()
        for k, fold in far_order:
            first_copy(q, k, fold).wait_send()
            second_copy(q, k, fold).wait_send()
            sg_copy(q, k, fold, 0).wait_send()
            fg_copy(q, k, fold, 0).wait_send()
        for k in range(1, NZ):
            z_copy(q, k).wait_send()
            zg_copy(q, k, 0).wait_send()
        for k, fold in order:
            cg_copy(q, k, fold).wait_send()

    def take_gathered(q):
        for k, fold in order:
            cg_copy(q, k, fold).wait_recv()
        for n in range(len(order)):
            core_copy(q, n).wait_send()

    def on_core(which, action, *given):
        @pl.when(core == which)
        def _():
            action(*given)

    loads[0].wait()
    loads[1].wait()
    unit, inverse = project(cf[...], iw[...])
    unit_c[...] = unit
    inv_c[...] = inverse
    corp[z] = unit.astype(bf16).reshape(2, TOK, E)
    pl.semaphore_wait(barrier, len(greeted))

    def z_send(buf, at, s, e, way, send_sem, recv_sem):
        send(buf.at[at, e], buf.at[at, e], send_sem.at[way, s - 1, e], recv_sem.at[way, s - 1, e], z_peers[way])

    def source(way, s):
        return (z + NZ - s) % NZ if way == 0 else (z + s) % NZ

    def z_step(buf, s, send_sem, recv_sem, work=()):
        work = list(work)
        for e in (0, 1):
            for way in (0, 1):
                if s == 8 and e != way:
                    continue
                at = source(way, s)
                arrived(buf.at[at, e], send_sem.at[way, s - 1, e], recv_sem.at[way, s - 1, e], z_peers[way])
                if s < 7 or (s == 7 and e == way):
                    z_send(buf, at, s + 1, e, way, send_sem, recv_sem)
                if work:
                    work.pop(0)()
        for piece in work:
            piece()

    for e in (0, 1):
        for way in (0, 1):
            z_send(corp, z, 1, e, way, zc_send, zc_recv)
    for load in loads[5:]:
        load.wait()
    code = owner_own[...] * OWN + row_own[...]
    codes[dev] = jnp.concatenate([code, code], axis=0)
    ids[group] = jnp.broadcast_to(ids_own[...], (8, TOK))
    send(codes.at[dev], pair_codes, pair_send, pair_recv, y_partner)

    loads[2].wait()
    loads[3].wait()
    unit, inverse = project(uf[...], uw[...])
    unit_u[...] = unit
    inv_u[...] = inverse
    user_low = unit.astype(bf16)
    cyc[group, 0] = user_low
    gus[z, y_lo] = user_low
    loads[4].wait()
    unit, inverse = project(itf[...], iw[...])
    unit_i[...] = unit
    inv_i[...] = inverse
    item_low = unit.astype(bf16)
    cyc[group, 1] = item_low
    far_group = lax.rem(group + NG // 2, NG)
    send(cyc.at[group], cyc.at[group], yh_send, yh_recv, y_far)
    for k in range(1, NX):
        send(cyc.at[group], cyc.at[group], x_send.at[0, k - 1], x_recv.at[0, k - 1], x_peers[k - 1])
    send(gus.at[z, y_lo], gus.at[z, y_lo], yu_send, yu_recv, y_partner)
    send(cyc.at[group], cyc.at[group], c_send.at[0, 0], c_recv.at[0, 0], sibling)

    def group_of(far, k, other):
        row = y_hi + far * (1 - 2 * y_hi)
        return (row * NX + (x + NX - k) % NX) * 2 + core + other * (1 - 2 * core)

    arrived(pair_codes, pair_send, pair_recv, y_partner)
    own_codes, their_codes = codes[dev], pair_codes[...]
    code_row = jnp.concatenate(
        [own_codes[n : n + 1] for n in range(4)] + [their_codes[n : n + 1] for n in range(4)], axis=1
    )
    wide_rows = lax.broadcasted_iota(jnp.int32, (OWN, 2 * NEG), 0)

    def select_from(at):
        hot = (code_row - (at * 2 + y_lo) * OWN == wide_rows).astype(f32).astype(bf16)
        return dot(corp[at].reshape(OWN, E), hot, 0, 0)

    def nothing():
        pass

    def select_more(way, s):
        def piece():
            select[...] += select_from(source(way, s))

        return piece

    code_rows = lax.broadcasted_iota(jnp.int32, (OWN, NEG), 0) + dev * OWN
    ones = jnp.ones((NEG, 128), bf16)

    def count_named(holder, carry):
        named = codes[holder]
        row = jnp.concatenate([named[n : n + 1] for n in range(4)], axis=1)
        counts[holder] = dot((row == code_rows).astype(f32).astype(bf16), ones).astype(bf16)
        return carry

    def count_piece(first, last):
        return lambda: lax.fori_loop(first, last, count_named, 0, unroll=2)

    select[...] = select_from(z)
    for s in range(1, 9):
        work = [nothing, select_more(0, s - 1), nothing, select_more(1, s - 1)] if s > 1 else []
        if 5 <= s <= 7:
            work[0] = count_piece(12 * s - 60, 12 * s - 54)
            work[2] = count_piece(12 * s - 54, min(12 * s - 48, ND))
        z_step(corp, s, zc_send, zc_recv, work)
        if s == 1:
            for k in range(1, ND):
                send(codes.at[dev], codes.at[dev], codes_send.at[k - 1], codes_recv.at[k - 1], dev_peers[k - 1])
        if s == 2:
            arrived(cyc.at[far_group], yh_send, yh_recv, y_far)
            for k in range(1, NX):
                send(cyc.at[far_group], cyc.at[far_group], x_send.at[1, k - 1], x_recv.at[1, k - 1], x_peers[k - 1])
            send(cyc.at[far_group], cyc.at[far_group], c_send.at[1, 0], c_recv.at[1, 0], sibling)
        if s == 3:
            for k in range(1, NG):
                send(ids.at[group], ids.at[group], ids_send.at[k - 1], ids_recv.at[k - 1], group_peers[k - 1])
        if s in (4, 6):
            far = (s - 4) // 2
            for k in range(1, NX):
                block = cyc.at[group_of(far, k, 0)]
                arrived(block, x_send.at[far, k - 1], x_recv.at[far, k - 1], x_peers[k - 1])
                send(block, block, c_send.at[far, k], c_recv.at[far, k], sibling)
        if s == 4:
            for k in range(1, ND):
                at = lax.rem(dev + ND - k, ND)
                arrived(codes.at[at], codes_send.at[k - 1], codes_recv.at[k - 1], dev_peers[k - 1])
        if s == 7:
            arrived(gus.at[z, 1 - y_lo], yu_send, yu_recv, y_partner)
            for e in (0, 1):
                for way in (0, 1):
                    z_send(gus, z, 1, e, way, zu_send, zu_recv)
    select[...] += select_from(source(0, 8))
    sel_out[...] = select[:, NEG:].astype(bf16)
    send(sel_out, sel_in, ys_send, ys_recv, y_partner)

    for far in (0, 1):
        for k in range(NX):
            arrived(cyc.at[group_of(far, k, 1)], c_send.at[far, k], c_recv.at[far, k], sibling)
    for k in range(1, NG):
        arrived(ids.at[lax.rem(group + NG - k, NG)], ids_send.at[k - 1], ids_recv.at[k - 1], group_peers[k - 1])

    tile_rows = lax.broadcasted_iota(jnp.int32, (TOK, TOK), 0)
    tile_columns = lax.broadcasted_iota(jnp.int32, (TOK, TOK), 1)
    eye = tile_rows == tile_columns

    def to_row(column):
        return jnp.sum(jnp.where(eye, column, 0.0), axis=0, keepdims=True)

    own_ids = ids_own[...].astype(f32)
    ids_column = jnp.sum(jnp.where(eye, own_ids, 0.0), axis=1, keepdims=True)
    user_low = cyc[group, 0]
    item_low = cyc[group, 1]

    wide_columns = lax.broadcasted_iota(jnp.int32, (TOK, QUAD * TOK), 1)
    own_column = lax.broadcasted_iota(jnp.int32, (TOK, QUAD * TOK), 0) + group * TOK

    def side(n, which):
        return cyc[QUAD * n : QUAD * n + QUAD, which].reshape(QUAD * TOK, E)

    def row_of(tiles, n):
        return jnp.concatenate([tiles[QUAD * n + i, 0:1] for i in range(QUAD)], axis=1)

    def diagonal_of(n):
        return wide_columns + n * QUAD * TOK == own_column

    def masks(n):
        diagonal = diagonal_of(n)
        same = row_of(ids, n).astype(f32) == ids_column
        return diagonal, jnp.logical_and(same, jnp.logical_not(diagonal))

    def folded(wide):
        return sum(wide[:, i * TOK : i * TOK + TOK] for i in range(QUAD))

    def forward_piece(n):
        def piece():
            logit = sharpen * dot(user_low, side(n, 1), 1, 1)
            diagonal, hidden = masks(n)
            value = jnp.where(hidden, 0.0, jnp.exp(logit))
            cexp[n] = value
            sums[...] += folded(value)
            own_sums[...] += folded(jnp.where(diagonal, logit, 0.0))

        return piece

    sums[...] = jnp.zeros((TOK, TOK), f32)
    own_sums[...] = jnp.zeros((TOK, TOK), f32)
    z_step(gus, 1, zu_send, zu_recv, [forward_piece(n) for n in range(4)])
    arrived(sel_in, ys_send, ys_recv, y_partner)
    sample_low = (select[:, :NEG] + sel_in[...].astype(f32)).astype(bf16)
    sample_exp = jnp.exp(sharpen * dot(user_low, sample_low))
    total = jnp.sum(sums[...], axis=1, keepdims=True) + jnp.sum(sample_exp, axis=1, keepdims=True)
    total_row = to_row(total)
    tot_g[group] = jnp.broadcast_to(total_row, (8, TOK))
    tot_d[dev] = jnp.broadcast_to(total_row, (8, TOK))
    for k in range(1, ND):
        send(tot_d.at[dev], tot_d.at[dev], td_send.at[k - 1], td_recv.at[k - 1], dev_peers[k - 1])
    for k in range(1, NG):
        send(tot_g.at[group], tot_g.at[group], tg_send.at[k - 1], tg_recv.at[k - 1], group_peers[k - 1])
    own_logit = jnp.sum(own_sums[...], axis=1, keepdims=True)
    loss_ref[...] = jnp.broadcast_to(to_row(jnp.log(total) - own_logit), (8, TOK))
    inverse_total = 1.0 / total
    sample_grad = (sample_exp * inverse_total * factor).astype(bf16)

    def user_piece(n):
        def piece():
            start = upward[...] if n else dot(sample_grad, sample_low, 1, 1)
            grad = ((cexp[n] * inverse_total - diagonal_of(n).astype(f32)) * factor).astype(bf16)
            upward[...] = start + dot(grad, side(n, 1))

        return piece

    z_step(gus, 2, zu_send, zu_recv, [user_piece(n) for n in range(4)])
    user_back = unnormalize(unit_u[...], inv_u[...], upward[...])

    def user_part(n):
        rows = order_rows(n)
        mine[0, rows] = dot(uf[:, rows], user_back, 0, 0)
        on_core(1, lambda: core_copy(0, n).start())

    def user_parts(n):
        def piece():
            user_part(2 * n)
            user_part(2 * n + 1)

        return piece

    z_step(gus, 3, zu_send, zu_recv, [user_parts(n) for n in range(4)])
    for k in range(1, NG):
        arrived(tot_g.at[lax.rem(group + NG - k, NG)], tg_send.at[k - 1], tg_recv.at[k - 1], group_peers[k - 1])

    def item_piece(n):
        def piece():
            users = side(n, 0)
            diagonal, hidden = masks(n)
            value = jnp.where(hidden, 0.0, jnp.exp(sharpen * dot(item_low, users, 1, 1)))
            grad = ((value * (1.0 / row_of(tot_g, n)) - diagonal.astype(f32)) * factor).astype(bf16)
            up = dot(grad, users)
            upward[...] = upward[...] + up if n else up

        return piece

    z_step(gus, 4, zu_send, zu_recv, [item_piece(n) for n in range(4)])
    item_back = unnormalize(unit_i[...], inv_i[...], upward[...])
    mine[1] = dot(itf[...], item_back, 0, 0)
    on_core(0, reduce_first, 0)
    for k in range(1, ND):
        at = lax.rem(dev + ND - k, ND)
        arrived(tot_d.at[at], td_send.at[k - 1], td_recv.at[k - 1], dev_peers[k - 1])
    owned[...] = jnp.zeros((OWN, E), f32)
    corpus_low = corp[z].reshape(OWN, E)

    def corpus_backward(at):
        users = gus[at].reshape(2 * TOK, E)
        value = jnp.exp(sharpen * dot(corpus_low, users, 1, 1))
        holder = at * 2
        scale = 1.0 / jnp.concatenate([tot_d[holder, 0:1], tot_d[holder + 1, 0:1]], axis=1)
        named = jnp.concatenate([counts[holder], counts[holder + 1]], axis=1).astype(f32)
        return dot((value * scale * factor * named).astype(bf16), users)

    def corpus_piece(*ats):
        def piece():
            owned[...] += sum(corpus_backward(at) for at in ats)

        return piece

    def both(s):
        return source(0, s), source(1, s)

    z_step(gus, 5, zu_send, zu_recv, [corpus_piece(z, source(0, 1)), corpus_piece(source(1, 1), source(0, 2)),
                                      corpus_piece(source(1, 2), source(0, 3)), corpus_piece(source(1, 3))])
    on_core(0, reduce_second, 0)
    z_step(gus, 6, zu_send, zu_recv, [corpus_piece(*both(4)), nothing, corpus_piece(*both(5)), nothing])
    on_core(0, reduce_z, 0)
    z_step(gus, 7, zu_send, zu_recv, [nothing, corpus_piece(*both(6))])
    z_step(gus, 8, zu_send, zu_recv, [corpus_piece(*both(7))])
    corpus_piece(source(0, 8))()
    owned_back = (owned[...] - unit_c[...] * jnp.sum(unit_c[...] * owned[...], axis=-1, keepdims=True)) * inv_c[...]
    high = owned_back.astype(bf16)
    low = (owned_back - high.astype(f32)).astype(bf16)
    for n in range(len(order)):
        rows = order_rows(n)
        mine[1, rows] += dot(cf[:, rows], high, 0, 0) + dot(cf[:, rows], low, 0, 0)
        on_core(0, lambda: core_copy(1, n).start())
    on_core(1, reduce_first, 1)
    on_core(1, reduce_second, 1)
    on_core(1, reduce_z, 1)
    on_core(1, gather_z, 1)
    on_core(1, gather_rest, 1)
    on_core(0, gather_z, 0)
    on_core(0, gather_rest, 0)
    on_core(1, take_gathered, 0)
    on_core(0, take_gathered, 1)
    for copy in sends:
        copy.wait_send()


def step(user_feat, item_feat, corpus_feat, user_weight, item_weight, ids, owners, rows):
    dma, vmem = pltpu.SemaphoreType.DMA, pltpu.VMEM
    pairs = lambda *shape: [dma(shape), dma(shape)]
    return pl.pallas_call(
        step_kernel,
        out_shape=[jax.ShapeDtypeStruct((8, TOK), f32), jax.ShapeDtypeStruct((2, WIDE, E), f32)],
        in_specs=[pl.BlockSpec(memory_space=pl.ANY)] * 8,
        out_specs=[pl.BlockSpec(memory_space=pltpu.VMEM)] * 2,
        scratch_shapes=[
            vmem((TOK, WIDE), bf16), vmem((TOK, WIDE), bf16), vmem((OWN, WIDE), bf16),
            vmem((WIDE, E), bf16), vmem((WIDE, E), bf16),
            vmem((1, TOK), jnp.int32), vmem((4, 128), jnp.int32), vmem((4, 128), jnp.int32),
            vmem((NZ, 2, TOK, E), bf16), vmem((NZ, 2, TOK, E), bf16), vmem((NG, 2, TOK, E), bf16),
            vmem((NG, 8, 128), jnp.int32), vmem((ND, 8, 128), jnp.int32), vmem((8, 128), jnp.int32),
            vmem((NG, 8, 128), f32), vmem((ND, 8, 128), f32),
            vmem((E, 2 * NEG), f32), vmem((E, NEG), bf16), vmem((E, NEG), bf16), vmem((NG // QUAD, TOK, QUAD * TOK), f32), vmem((ND, OWN, 128), bf16),
            vmem((TOK, TOK), f32), vmem((TOK, TOK), f32),
            vmem((TOK, E), f32), vmem((TOK, E), f32), vmem((OWN, E), f32),
            vmem((TOK, 1), f32), vmem((TOK, 1), f32), vmem((OWN, 1), f32), vmem((TOK, E), f32), vmem((OWN, E), f32),
            vmem((2, WIDE, E), f32), vmem((8, PART, E), f32), vmem((2, 3, PART, E), f32), vmem((2, 3, BIT, E), f32),
            vmem((NZ - 1, 8, 128), f32),
            dma((8,)), *pairs(NG - 1), *pairs(ND - 1), *pairs(), *pairs(NG - 1), *pairs(ND - 1),
            *pairs(2, 8, 2), *pairs(2, 8, 2), *pairs(), *pairs(), *pairs(), *pairs(2, 3), *pairs(2, 4),
            *pairs(8), *pairs(2, 3), *pairs(2, 3), *pairs(NZ - 1), *pairs(NZ - 1), *pairs(2, 3), *pairs(2, 3),
            *pairs(2, 4),
        ],
        compiler_params=pltpu.CompilerParams(
            collective_id=0, has_side_effects=True, vmem_limit_bytes=60 * 1024 * 1024
        ),
        name="step",
    )(user_feat, item_feat, corpus_feat, user_weight, item_weight, ids, owners, rows)


def local(
    user_feat, item_feat, item_ids, corpus_feat, neg_owner, neg_row, user_weight, item_weight
):
    loss, grads = step(
        user_feat, item_feat, corpus_feat, user_weight, item_weight,
        item_ids.reshape(1, TOK), neg_owner.reshape(4, 128), neg_row.reshape(4, 128),
    )
    return loss[0], grads[0], grads[1]


def solution(mesh):
    return jax.shard_map(
        local,
        mesh=mesh,
        in_specs=(
            P(("group", "dev"), None),
            P(("group", "dev"), None),
            P(("group", "dev")),
            P(("group", "dev"), None),
            P(("group", "dev"), None),
            P(("group", "dev")),
            P(),
            P(),
        ),
        out_specs=(P(("group", "dev")), P(), P()),
        check_vma=False,
    )
```

```python
import jax
import jax.numpy as jnp
from jax import lax
from jax.experimental import pallas as pl
from jax.experimental.pallas import tpu as pltpu
from jax.sharding import PartitionSpec as P

sharpen = 20.0
epsilon = 1e-06
MESH = pl.DeviceIdType.MESH
NX, NY, NZ = 4, 4, 16


def place():
    group, dev = lax.axis_index("group"), lax.axis_index("dev")
    core, x, y_hi = group % 2, (group // 2) % NX, group // (2 * NX)
    z, y_lo = dev // 2, dev % 2
    return core, x, y_hi * 2 + y_lo, z


def device_at(core, x, y, z):
    return (((y // 2) * NX + x) * 2 + core, z * 2 + y % 2)


def greet(partners):
    barrier = pltpu.get_barrier_semaphore()
    for partner in partners:
        pl.semaphore_signal(barrier, inc=1, device_id=partner, device_id_type=MESH)
    pl.semaphore_wait(barrier, len(partners))


def remote(src, dst, send_sem, recv_sem, device):
    return pltpu.make_async_remote_copy(
        src_ref=src, dst_ref=dst, send_sem=send_sem, recv_sem=recv_sem, device_id=device, device_id_type=MESH
    )


TOK, OWN, NEG, WIDE, E = 128, 256, 512, 1024, 256
NG, ND = 16, 32
QUAD = 4
f32, bf16 = jnp.float32, jnp.bfloat16


def dot(left, right, left_dim=1, right_dim=0):
    return lax.dot_general(left, right, (((left_dim,), (right_dim,)), ((), ())), preferred_element_type=f32)


def project(features, weight):
    hidden = dot(features, weight)
    inverse = lax.rsqrt(jnp.sum(hidden * hidden, axis=-1, keepdims=True) + epsilon)
    return hidden * inverse, inverse


def unnormalize(unit, inverse, upstream):
    along = jnp.sum(unit * upstream, axis=-1, keepdims=True)
    return ((upstream - unit * along) * inverse).astype(bf16)


FOLD = 512
PART = 128
BIT = 32


def step_kernel(
    user_feat, item_feat, corpus_feat, user_weight, item_weight, ids_in, owner_in, row_in,
    loss_ref, out_ref,
    uf, itf, cf, uw, iw, ids_own, owner_own, row_own, corp, gus, cyc, ids, codes, pair_codes, tot_g, tot_d,
    select, sel_out, sel_in, cexp, counts, sums, own_sums, unit_u, unit_i, unit_c, inv_u, inv_i, inv_c, upward, owned,
    mine, from_core, from_first, from_second, from_z,
    load_sem, ids_send, ids_recv, codes_send, codes_recv, pair_send, pair_recv, tg_send, tg_recv, td_send, td_recv,
    zc_send, zc_recv, zu_send, zu_recv, yu_send, yu_recv, ys_send, ys_recv,
    yh_send, yh_recv, x_send, x_recv, c_send, c_recv,
    core_send, core_recv, first_send, first_recv, second_send, second_recv, z_sends, z_recvs,
    zg_send, zg_recv, sg_send, sg_recv, fg_send, fg_recv, cg_send, cg_recv,
):
    core, x, y, z = place()
    y_hi, y_lo = y // 2, y % 2
    group, dev = lax.axis_index("group"), lax.axis_index("dev")
    factor = sharpen / TOK
    loads = [
        pltpu.make_async_copy(src, dst, load_sem.at[n])
        for n, (src, dst) in enumerate([
            (corpus_feat, cf), (item_weight, iw), (user_feat, uf), (user_weight, uw), (item_feat, itf),
            (ids_in, ids_own), (owner_in, owner_own), (row_in, row_own),
        ])
    ]
    for load in loads:
        load.start()
    group_peers = [(lax.rem(group + k, NG), dev) for k in range(1, NG)]
    dev_peers = [(group, lax.rem(dev + k, ND)) for k in range(1, ND)]
    sibling = device_at(1 - core, x, y, z)
    y_partner = device_at(core, x, y_hi * 2 + 1 - y_lo, z)
    y_far = device_at(core, x, (1 - y_hi) * 2 + y_lo, z)
    x_peers = [device_at(core, (x + k) % NX, y, z) for k in range(1, NX)]
    y_peers = [device_at(core, x, (y + k) % NY, z) for k in range(1, NY)]
    z_all = [device_at(core, x, y, (z + k) % NZ) for k in range(1, NZ)]
    z_peers = [z_all[0], z_all[-1]]
    sends = []

    def send(src, dst, send_sem, recv_sem, device):
        copy = remote(src, dst, send_sem, recv_sem, device)
        copy.start()
        sends.append(copy)

    def arrived(dst, send_sem, recv_sem, device):
        remote(dst, dst, send_sem, recv_sem, device).wait_recv()

    barrier = pltpu.get_barrier_semaphore()
    greeted = group_peers + dev_peers + [device_at(core, x, NY - 1 - y, z)]
    for partner in greeted:
        pl.semaphore_signal(barrier, inc=1, device_id=partner, device_id_type=MESH)

    first_at, second_at = [x, y], [y, x]
    along = [x_peers, y_peers]

    def part_rows(fold, part):
        return pl.ds(pl.multiple_of(fold * FOLD + part * PART, PART), PART)

    def bit_rows(fold, part, bit):
        return pl.ds(pl.multiple_of(fold * FOLD + part * PART + bit * BIT, BIT), BIT)

    def tile_of(at):
        fold = at // 8
        row = fold * FOLD + (x + fold * (y - x)) * PART + (y + fold * (x - y)) * BIT + ((at // 2) % 4) * 8
        return pl.ds(pl.multiple_of(row, 8), 8), pl.ds(pl.multiple_of((at % 2) * 128, 128), 128)

    order = [(k, fold) for k in (1, 2, 3, 0) for fold in (0, 1)]
    far_order = [(k, fold) for k in (1, 2, 3) for fold in (0, 1)]

    def order_rows(n):
        k, fold = order[n]
        return part_rows(fold, (first_at[fold] + k) % 4)

    def core_copy(q, n):
        return remote(mine.at[q, order_rows(n)], from_core.at[n], core_send.at[n], core_recv.at[n], sibling)

    def first_copy(q, k, fold):
        rows = part_rows(fold, (first_at[fold] + k) % 4)
        return remote(
            mine.at[q, rows], from_first.at[fold, k - 1], first_send.at[fold, k - 1], first_recv.at[fold, k - 1],
            along[fold][k - 1],
        )

    def second_copy(q, k, fold):
        rows = bit_rows(fold, first_at[fold], (second_at[fold] + k) % 4)
        return remote(
            mine.at[q, rows], from_second.at[fold, k - 1], second_send.at[fold, k - 1], second_recv.at[fold, k - 1],
            along[1 - fold][k - 1],
        )

    def z_copy(q, k):
        rows, columns = tile_of((z + k) % NZ)
        return remote(mine.at[q, rows, columns], from_z.at[k - 1], z_sends.at[k - 1], z_recvs.at[k - 1], z_all[k - 1])

    def zg_copy(q, k, back):
        rows, columns = tile_of((z + NZ - k * back) % NZ)
        tile = out_ref.at[q, rows, columns]
        return remote(tile, tile, zg_send.at[k - 1], zg_recv.at[k - 1], z_all[k - 1])

    def sg_copy(q, k, fold, back):
        bit = out_ref.at[q, bit_rows(fold, first_at[fold], (second_at[fold] + 4 - k * back) % 4)]
        return remote(bit, bit, sg_send.at[fold, k - 1], sg_recv.at[fold, k - 1], along[1 - fold][k - 1])

    def fg_copy(q, k, fold, back):
        part = out_ref.at[q, part_rows(fold, (first_at[fold] + 4 - k * back) % 4)]
        return remote(part, part, fg_send.at[fold, k - 1], fg_recv.at[fold, k - 1], along[fold][k - 1])

    def cg_copy(q, k, fold):
        part = out_ref.at[q, part_rows(fold, (first_at[fold] + 4 - k) % 4)]
        return remote(part, part, cg_send.at[fold, k], cg_recv.at[fold, k], sibling)

    def reduce_first(q):
        for n, (k, fold) in enumerate(order):
            rows = order_rows(n)
            core_copy(q, n).wait_recv()
            mine[q, rows] += from_core[n]
            if k:
                first_copy(q, k, fold).start()

    def reduce_second(q):
        for k, fold in far_order:
            first_copy(q, k, fold).wait_recv()
        for k, fold in order:
            at = (second_at[fold] + k) % 4
            rows = bit_rows(fold, first_at[fold], at)
            near = pl.ds(pl.multiple_of(at * BIT, BIT), BIT)
            mine[q, rows] += from_first[fold, 0, near] + from_first[fold, 1, near] + from_first[fold, 2, near]
            if k:
                second_copy(q, k, fold).start()

    def reduce_z(q):
        for k, fold in far_order:
            second_copy(q, k, fold).wait_recv()
        for fold in (0, 1):
            rows = bit_rows(fold, first_at[fold], second_at[fold])
            mine[q, rows] += from_second[fold, 0] + from_second[fold, 1] + from_second[fold, 2]
        for k in range(1, NZ):
            z_copy(q, k).start()

    def gather_z(q):
        rows, columns = tile_of(z)
        total = mine[q, rows, columns]
        for k in range(1, NZ):
            z_copy(q, k).wait_recv()
            total = total + from_z[k - 1]
        out_ref[q, rows, columns] = total
        for k in range(1, NZ):
            zg_copy(q, k, 0).start()

    def gather_rest(q):
        for k in range(1, NZ):
            zg_copy(q, k, 1).wait_recv()
        for k, fold in far_order:
            sg_copy(q, k, fold, 0).start()
        for k, fold in far_order:
            sg_copy(q, k, fold, 1).wait_recv()
        for k, fold in far_order:
            fg_copy(q, k, fold, 0).start()
        for fold in (0, 1):
            cg_copy(q, 0, fold).start()
        for k, fold in far_order:
            fg_copy(q, k, fold, 1).wait_recv()
            cg_copy(q, k, fold).start()
        for k, fold in far_order:
            first_copy(q, k, fold).wait_send()
            second_copy(q, k, fold).wait_send()
            sg_copy(q, k, fold, 0).wait_send()
            fg_copy(q, k, fold, 0).wait_send()
        for k in range(1, NZ):
            z_copy(q, k).wait_send()
            zg_copy(q, k, 0).wait_send()
        for k, fold in order:
            cg_copy(q, k, fold).wait_send()

    def take_gathered(q):
        for k, fold in order:
            cg_copy(q, k, fold).wait_recv()
        for n in range(len(order)):
            core_copy(q, n).wait_send()

    def on_core(which, action, *given):
        @pl.when(core == which)
        def _():
            action(*given)

    loads[0].wait()
    loads[1].wait()
    unit, inverse = project(cf[...], iw[...])
    unit_c[...] = unit
    inv_c[...] = inverse
    corp[z] = unit.astype(bf16).reshape(2, TOK, E)
    pl.semaphore_wait(barrier, len(greeted))

    def z_send(buf, at, s, e, way, send_sem, recv_sem):
        send(buf.at[at, e], buf.at[at, e], send_sem.at[way, s - 1, e], recv_sem.at[way, s - 1, e], z_peers[way])

    def source(way, s):
        return (z + NZ - s) % NZ if way == 0 else (z + s) % NZ

    def corpus_step(s, work):
        for e in (0, 1):
            for way in (0, 1):
                if s < 8 or e == way:
                    at = source(way, s)
                    arrived(corp.at[at, e], zc_send.at[way, s - 1, e], zc_recv.at[way, s - 1, e], z_peers[way])
                    if s < 7 or (s == 7 and e == way):
                        z_send(corp, at, s + 1, e, way, zc_send, zc_recv)
                if work:
                    work.pop(0)()

    def user_send(at, s, way):
        block = gus.at[at, y_lo]
        send(block, block, zu_send.at[way, s - 1], zu_recv.at[way, s - 1], z_peers[way])

    def user_step(s):
        for way in (0, 1) if s < 8 else (0,):
            at = source(way, s)
            block = gus.at[at, y_lo]
            arrived(block, zu_send.at[way, s - 1], zu_recv.at[way, s - 1], z_peers[way])
            if s < 7 or (s == 7 and way == 0):
                user_send(at, s + 1, way)
            send(block, block, yu_send.at[way, s], yu_recv.at[way, s], y_partner)

    def users_handed(s):
        for way in (0, 1) if 0 < s < 8 else (0,):
            block = gus.at[source(way, s), 1 - y_lo]
            arrived(block, yu_send.at[way, s], yu_recv.at[way, s], y_partner)

    for e in (0, 1):
        for way in (0, 1):
            z_send(corp, z, 1, e, way, zc_send, zc_recv)
    for load in loads[5:]:
        load.wait()
    code = owner_own[...] * OWN + row_own[...]
    codes[dev] = jnp.concatenate([code, code], axis=0)
    ids[group] = jnp.broadcast_to(ids_own[...], (8, TOK))
    send(codes.at[dev], pair_codes, pair_send, pair_recv, y_partner)

    loads[2].wait()
    loads[3].wait()
    unit, inverse = project(uf[...], uw[...])
    unit_u[...] = unit
    inv_u[...] = inverse
    user_low = unit.astype(bf16)
    cyc[group, 0] = user_low
    gus[z, y_lo] = user_low
    for way in (0, 1):
        user_send(z, 1, way)
    send(gus.at[z, y_lo], gus.at[z, y_lo], yu_send.at[0, 0], yu_recv.at[0, 0], y_partner)
    loads[4].wait()
    unit, inverse = project(itf[...], iw[...])
    unit_i[...] = unit
    inv_i[...] = inverse
    item_low = unit.astype(bf16)
    cyc[group, 1] = item_low
    far_group = lax.rem(group + NG // 2, NG)
    send(cyc.at[group], cyc.at[group], yh_send, yh_recv, y_far)
    for k in range(1, NX):
        send(cyc.at[group], cyc.at[group], x_send.at[0, k - 1], x_recv.at[0, k - 1], x_peers[k - 1])
    send(cyc.at[group], cyc.at[group], c_send.at[0, 0], c_recv.at[0, 0], sibling)

    def group_of(far, k, other):
        row = y_hi + far * (1 - 2 * y_hi)
        return (row * NX + (x + NX - k) % NX) * 2 + core + other * (1 - 2 * core)

    arrived(pair_codes, pair_send, pair_recv, y_partner)
    own_codes, their_codes = codes[dev], pair_codes[...]
    code_row = jnp.concatenate(
        [own_codes[n : n + 1] for n in range(4)] + [their_codes[n : n + 1] for n in range(4)], axis=1
    )
    wide_rows = lax.broadcasted_iota(jnp.int32, (OWN, 2 * NEG), 0)

    def select_from(at):
        hot = (code_row - (at * 2 + y_lo) * OWN == wide_rows).astype(f32).astype(bf16)
        return dot(corp[at].reshape(OWN, E), hot, 0, 0)

    def nothing():
        pass

    def select_more(way, s):
        def piece():
            select[...] += select_from(source(way, s))

        return piece

    code_rows = lax.broadcasted_iota(jnp.int32, (OWN, NEG), 0) + dev * OWN
    ones = jnp.ones((NEG, 128), bf16)

    def count_named(holder, carry):
        named = codes[holder]
        row = jnp.concatenate([named[n : n + 1] for n in range(4)], axis=1)
        counts[holder] = dot((row == code_rows).astype(f32).astype(bf16), ones).astype(bf16)
        return carry

    def count_piece(first, last):
        return lambda: lax.fori_loop(first, last, count_named, 0, unroll=2)

    select[...] = select_from(z)
    for s in range(1, 9):
        work = [nothing, select_more(0, s - 1), nothing, select_more(1, s - 1)] if s > 1 else []
        if 5 <= s <= 7:
            work[0] = count_piece(12 * s - 60, 12 * s - 54)
            work[2] = count_piece(12 * s - 54, min(12 * s - 48, ND))
        corpus_step(s, work)
        user_step(s)
        if s == 1:
            for k in range(1, ND):
                send(codes.at[dev], codes.at[dev], codes_send.at[k - 1], codes_recv.at[k - 1], dev_peers[k - 1])
        if s == 2:
            arrived(cyc.at[far_group], yh_send, yh_recv, y_far)
            for k in range(1, NX):
                send(cyc.at[far_group], cyc.at[far_group], x_send.at[1, k - 1], x_recv.at[1, k - 1], x_peers[k - 1])
            send(cyc.at[far_group], cyc.at[far_group], c_send.at[1, 0], c_recv.at[1, 0], sibling)
        if s == 3:
            for k in range(1, NG):
                send(ids.at[group], ids.at[group], ids_send.at[k - 1], ids_recv.at[k - 1], group_peers[k - 1])
        if s in (4, 6):
            far = (s - 4) // 2
            for k in range(1, NX):
                block = cyc.at[group_of(far, k, 0)]
                arrived(block, x_send.at[far, k - 1], x_recv.at[far, k - 1], x_peers[k - 1])
                send(block, block, c_send.at[far, k], c_recv.at[far, k], sibling)
        if s == 4:
            for k in range(1, ND):
                at = lax.rem(dev + ND - k, ND)
                arrived(codes.at[at], codes_send.at[k - 1], codes_recv.at[k - 1], dev_peers[k - 1])
    select[...] += select_from(source(0, 8))
    sel_out[...] = select[:, NEG:].astype(bf16)
    send(sel_out, sel_in, ys_send, ys_recv, y_partner)

    for far in (0, 1):
        for k in range(NX):
            arrived(cyc.at[group_of(far, k, 1)], c_send.at[far, k], c_recv.at[far, k], sibling)
    for k in range(1, NG):
        arrived(ids.at[lax.rem(group + NG - k, NG)], ids_send.at[k - 1], ids_recv.at[k - 1], group_peers[k - 1])

    tile_rows = lax.broadcasted_iota(jnp.int32, (TOK, TOK), 0)
    tile_columns = lax.broadcasted_iota(jnp.int32, (TOK, TOK), 1)
    eye = tile_rows == tile_columns

    def to_row(column):
        return jnp.sum(jnp.where(eye, column, 0.0), axis=0, keepdims=True)

    own_ids = ids_own[...].astype(f32)
    ids_column = jnp.sum(jnp.where(eye, own_ids, 0.0), axis=1, keepdims=True)
    user_low = cyc[group, 0]
    item_low = cyc[group, 1]

    wide_columns = lax.broadcasted_iota(jnp.int32, (TOK, QUAD * TOK), 1)
    own_column = lax.broadcasted_iota(jnp.int32, (TOK, QUAD * TOK), 0) + group * TOK

    def side(n, which):
        return cyc[QUAD * n : QUAD * n + QUAD, which].reshape(QUAD * TOK, E)

    def row_of(tiles, n):
        return jnp.concatenate([tiles[QUAD * n + i, 0:1] for i in range(QUAD)], axis=1)

    def diagonal_of(n):
        return wide_columns + n * QUAD * TOK == own_column

    def masks(n):
        diagonal = diagonal_of(n)
        same = row_of(ids, n).astype(f32) == ids_column
        return diagonal, jnp.logical_and(same, jnp.logical_not(diagonal))

    def folded(wide):
        return sum(wide[:, i * TOK : i * TOK + TOK] for i in range(QUAD))

    def forward_piece(n):
        def piece():
            logit = sharpen * dot(user_low, side(n, 1), 1, 1)
            diagonal, hidden = masks(n)
            value = jnp.where(hidden, 0.0, jnp.exp(logit))
            cexp[n] = value
            sums[...] += folded(value)
            own_sums[...] += folded(jnp.where(diagonal, logit, 0.0))

        return piece

    sums[...] = jnp.zeros((TOK, TOK), f32)
    own_sums[...] = jnp.zeros((TOK, TOK), f32)
    for n in range(NG // QUAD):
        forward_piece(n)()
    arrived(sel_in, ys_send, ys_recv, y_partner)
    sample_low = (select[:, :NEG] + sel_in[...].astype(f32)).astype(bf16)
    sample_exp = jnp.exp(sharpen * dot(user_low, sample_low))
    total = jnp.sum(sums[...], axis=1, keepdims=True) + jnp.sum(sample_exp, axis=1, keepdims=True)
    total_row = to_row(total)
    tot_g[group] = jnp.broadcast_to(total_row, (8, TOK))
    tot_d[dev] = jnp.broadcast_to(total_row, (8, TOK))
    for k in range(1, ND):
        send(tot_d.at[dev], tot_d.at[dev], td_send.at[k - 1], td_recv.at[k - 1], dev_peers[k - 1])
    for k in range(1, NG):
        send(tot_g.at[group], tot_g.at[group], tg_send.at[k - 1], tg_recv.at[k - 1], group_peers[k - 1])
    own_logit = jnp.sum(own_sums[...], axis=1, keepdims=True)
    loss_ref[...] = jnp.broadcast_to(to_row(jnp.log(total) - own_logit), (8, TOK))
    inverse_total = 1.0 / total
    sample_grad = (sample_exp * inverse_total * factor).astype(bf16)

    def user_piece(n):
        def piece():
            start = upward[...] if n else dot(sample_grad, sample_low, 1, 1)
            grad = ((cexp[n] * inverse_total - diagonal_of(n).astype(f32)) * factor).astype(bf16)
            upward[...] = start + dot(grad, side(n, 1))

        return piece

    for n in range(NG // QUAD):
        user_piece(n)()
    user_back = unnormalize(unit_u[...], inv_u[...], upward[...])

    def user_part(n):
        rows = order_rows(n)
        mine[0, rows] = dot(uf[:, rows], user_back, 0, 0)
        on_core(1, lambda: core_copy(0, n).start())

    def user_parts(n):
        def piece():
            user_part(2 * n)
            user_part(2 * n + 1)

        return piece

    for n in range(4):
        user_parts(n)()
    for k in range(1, NG):
        arrived(tot_g.at[lax.rem(group + NG - k, NG)], tg_send.at[k - 1], tg_recv.at[k - 1], group_peers[k - 1])

    def item_piece(n):
        def piece():
            users = side(n, 0)
            diagonal, hidden = masks(n)
            value = jnp.where(hidden, 0.0, jnp.exp(sharpen * dot(item_low, users, 1, 1)))
            grad = ((value * (1.0 / row_of(tot_g, n)) - diagonal.astype(f32)) * factor).astype(bf16)
            up = dot(grad, users)
            upward[...] = upward[...] + up if n else up

        return piece

    for n in range(NG // QUAD):
        item_piece(n)()
    item_back = unnormalize(unit_i[...], inv_i[...], upward[...])
    mine[1] = dot(itf[...], item_back, 0, 0)
    on_core(0, reduce_first, 0)
    for s in range(9):
        users_handed(s)
    for k in range(1, ND):
        at = lax.rem(dev + ND - k, ND)
        arrived(tot_d.at[at], td_send.at[k - 1], td_recv.at[k - 1], dev_peers[k - 1])
    owned[...] = jnp.zeros((OWN, E), f32)
    corpus_low = corp[z].reshape(OWN, E)

    def corpus_backward(at):
        users = gus[at].reshape(2 * TOK, E)
        value = jnp.exp(sharpen * dot(corpus_low, users, 1, 1))
        holder = at * 2
        scale = 1.0 / jnp.concatenate([tot_d[holder, 0:1], tot_d[holder + 1, 0:1]], axis=1)
        named = jnp.concatenate([counts[holder], counts[holder + 1]], axis=1).astype(f32)
        return dot((value * scale * factor * named).astype(bf16), users)

    def corpus_piece(*ats):
        def piece():
            owned[...] += sum(corpus_backward(at) for at in ats)

        return piece

    def both(s):
        return source(0, s), source(1, s)

    corpus_piece(z, source(0, 8))()
    for s in range(1, 8):
        corpus_piece(*both(s))()
    owned_back = (owned[...] - unit_c[...] * jnp.sum(unit_c[...] * owned[...], axis=-1, keepdims=True)) * inv_c[...]
    high = owned_back.astype(bf16)
    low = (owned_back - high.astype(f32)).astype(bf16)
    for n in range(len(order)):
        rows = order_rows(n)
        mine[1, rows] += dot(cf[:, rows], high, 0, 0) + dot(cf[:, rows], low, 0, 0)
        on_core(0, lambda: core_copy(1, n).start())
    on_core(1, reduce_first, 1)
    on_core(1, reduce_second, 1)
    on_core(1, reduce_z, 1)
    on_core(1, gather_z, 1)
    on_core(1, gather_rest, 1)
    on_core(0, reduce_second, 0)
    on_core(0, reduce_z, 0)
    on_core(0, gather_z, 0)
    on_core(0, gather_rest, 0)
    on_core(1, take_gathered, 0)
    on_core(0, take_gathered, 1)
    for copy in sends:
        copy.wait_send()


def step(user_feat, item_feat, corpus_feat, user_weight, item_weight, ids, owners, rows):
    dma, vmem = pltpu.SemaphoreType.DMA, pltpu.VMEM
    pairs = lambda *shape: [dma(shape), dma(shape)]
    return pl.pallas_call(
        step_kernel,
        out_shape=[jax.ShapeDtypeStruct((8, TOK), f32), jax.ShapeDtypeStruct((2, WIDE, E), f32)],
        in_specs=[pl.BlockSpec(memory_space=pltpu.HBM)] * 8,
        out_specs=[pl.BlockSpec(memory_space=pltpu.VMEM)] * 2,
        scratch_shapes=[
            vmem((TOK, WIDE), bf16), vmem((TOK, WIDE), bf16), vmem((OWN, WIDE), bf16),
            vmem((WIDE, E), bf16), vmem((WIDE, E), bf16),
            vmem((1, TOK), jnp.int32), vmem((4, 128), jnp.int32), vmem((4, 128), jnp.int32),
            vmem((NZ, 2, TOK, E), bf16), vmem((NZ, 2, TOK, E), bf16), vmem((NG, 2, TOK, E), bf16),
            vmem((NG, 8, 128), jnp.int32), vmem((ND, 8, 128), jnp.int32), vmem((8, 128), jnp.int32),
            vmem((NG, 8, 128), f32), vmem((ND, 8, 128), f32),
            vmem((E, 2 * NEG), f32), vmem((E, NEG), bf16), vmem((E, NEG), bf16), vmem((NG // QUAD, TOK, QUAD * TOK), f32), vmem((ND, OWN, 128), bf16),
            vmem((TOK, TOK), f32), vmem((TOK, TOK), f32),
            vmem((TOK, E), f32), vmem((TOK, E), f32), vmem((OWN, E), f32),
            vmem((TOK, 1), f32), vmem((TOK, 1), f32), vmem((OWN, 1), f32), vmem((TOK, E), f32), vmem((OWN, E), f32),
            vmem((2, WIDE, E), f32), vmem((8, PART, E), f32), vmem((2, 3, PART, E), f32), vmem((2, 3, BIT, E), f32),
            vmem((NZ - 1, 8, 128), f32),
            dma((8,)), *pairs(NG - 1), *pairs(ND - 1), *pairs(), *pairs(NG - 1), *pairs(ND - 1),
            *pairs(2, 8, 2), *pairs(2, 8), *pairs(2, 9), *pairs(), *pairs(), *pairs(2, 3), *pairs(2, 4),
            *pairs(8), *pairs(2, 3), *pairs(2, 3), *pairs(NZ - 1), *pairs(NZ - 1), *pairs(2, 3), *pairs(2, 3),
            *pairs(2, 4),
        ],
        compiler_params=pltpu.CompilerParams(
            collective_id=0, has_side_effects=True, vmem_limit_bytes=60 * 1024 * 1024
        ),
        name="step",
    )(user_feat, item_feat, corpus_feat, user_weight, item_weight, ids, owners, rows)


def local(
    user_feat, item_feat, item_ids, corpus_feat, neg_owner, neg_row, user_weight, item_weight
):
    loss, grads = step(
        user_feat, item_feat, corpus_feat, user_weight, item_weight,
        item_ids.reshape(1, TOK), neg_owner.reshape(4, 128), neg_row.reshape(4, 128),
    )
    return loss[0], grads[0], grads[1]


def solution(mesh):
    return jax.shard_map(
        local,
        mesh=mesh,
        in_specs=(
            P(("group", "dev"), None),
            P(("group", "dev"), None),
            P(("group", "dev")),
            P(("group", "dev"), None),
            P(("group", "dev"), None),
            P(("group", "dev")),
            P(),
            P(),
        ),
        out_specs=(P(("group", "dev")), P(), P()),
        check_vma=False,
    )
```

```python
import functools

import jax
import jax.numpy as jnp
from jax import lax
from jax.experimental import pallas as pl
from jax.experimental.pallas import tpu as pltpu
from jax.sharding import PartitionSpec as P

sharpen = 20.0
epsilon = 1e-06
MESH = pl.DeviceIdType.MESH
NX, NY, NZ = 4, 4, 16


def place():
    group, dev = lax.axis_index("group"), lax.axis_index("dev")
    core, x, y_hi = group % 2, (group // 2) % NX, group // (2 * NX)
    z, y_lo = dev // 2, dev % 2
    return core, x, y_hi * 2 + y_lo, z


def device_at(core, x, y, z):
    return (((y // 2) * NX + x) * 2 + core, z * 2 + y % 2)


def greet(partners):
    barrier = pltpu.get_barrier_semaphore()
    for partner in partners:
        pl.semaphore_signal(barrier, inc=1, device_id=partner, device_id_type=MESH)
    pl.semaphore_wait(barrier, len(partners))


def remote(src, dst, send_sem, recv_sem, device):
    return pltpu.make_async_remote_copy(
        src_ref=src, dst_ref=dst, send_sem=send_sem, recv_sem=recv_sem, device_id=device, device_id_type=MESH
    )


TOK, OWN, NEG, WIDE, E = 128, 256, 512, 1024, 256
NG, ND = 16, 32
QUAD = 4
f32, bf16 = jnp.float32, jnp.bfloat16


def dot(left, right, left_dim=1, right_dim=0):
    return lax.dot_general(left, right, (((left_dim,), (right_dim,)), ((), ())), preferred_element_type=f32)


def project(features, weight):
    hidden = dot(features, weight)
    inverse = lax.rsqrt(jnp.sum(hidden * hidden, axis=-1, keepdims=True) + epsilon)
    return hidden * inverse, inverse


def unnormalize(unit, inverse, upstream):
    along = jnp.sum(unit * upstream, axis=-1, keepdims=True)
    return ((upstream - unit * along) * inverse).astype(bf16)


FOLD = 512
PART = 128
BIT = 32


def step_kernel(
    user_feat, item_feat, corpus_feat, user_weight, item_weight, ids_in, owner_in, row_in,
    loss_ref, out_ref,
    uf, itf, cf, uw, iw, ids_own, owner_own, row_own, corp, gus, cyc, ids, codes, pair_codes, tot_g, tot_d,
    select, sel_out, sel_in, cexp, counts, sums, own_sums, unit_u, unit_i, unit_c, inv_u, inv_i, inv_c, upward, owned,
    mine, from_core, from_first, from_second, from_z,
    load_sem, ids_send, ids_recv, zn_send, zn_recv, yn_send, yn_recv, pair_send, pair_recv, tg_send, tg_recv, td_send, td_recv,
    zc_send, zc_recv, zu_send, zu_recv, yu_send, yu_recv, ys_send, ys_recv,
    yh_send, yh_recv, x_send, x_recv, c_send, c_recv,
    core_send, core_recv, first_send, first_recv, second_send, second_recv, z_sends, z_recvs,
    zg_send, zg_recv, sg_send, sg_recv, fg_send, fg_recv, cg_send, cg_recv,
):
    core, x, y, z = place()
    y_hi, y_lo = y // 2, y % 2
    group, dev = lax.axis_index("group"), lax.axis_index("dev")
    factor = sharpen / TOK
    loads = [
        pltpu.make_async_copy(src, dst, load_sem.at[n])
        for n, (src, dst) in enumerate([
            (corpus_feat, cf), (item_weight, iw), (user_feat, uf), (user_weight, uw), (item_feat, itf),
            (ids_in, ids_own), (owner_in, owner_own), (row_in, row_own),
        ])
    ]
    for load in loads:
        load.start()
    group_peers = [(lax.rem(group + k, NG), dev) for k in range(1, NG)]
    dev_peers = [(group, lax.rem(dev + k, ND)) for k in range(1, ND)]
    sibling = device_at(1 - core, x, y, z)
    y_partner = device_at(core, x, y_hi * 2 + 1 - y_lo, z)
    y_far = device_at(core, x, (1 - y_hi) * 2 + y_lo, z)
    x_peers = [device_at(core, (x + k) % NX, y, z) for k in range(1, NX)]
    y_peers = [device_at(core, x, (y + k) % NY, z) for k in range(1, NY)]
    z_all = [device_at(core, x, y, (z + k) % NZ) for k in range(1, NZ)]
    z_peers = [z_all[0], z_all[-1]]
    sends = []

    def send(src, dst, send_sem, recv_sem, device):
        copy = remote(src, dst, send_sem, recv_sem, device)
        copy.start()
        sends.append(copy)

    def arrived(dst, send_sem, recv_sem, device):
        remote(dst, dst, send_sem, recv_sem, device).wait_recv()

    barrier = pltpu.get_barrier_semaphore()
    greeted = [sibling] + x_peers + y_peers + z_peers
    for partner in greeted:
        pl.semaphore_signal(barrier, inc=1, device_id=partner, device_id_type=MESH)

    first_at, second_at = [x, y], [y, x]
    along = [x_peers, y_peers]

    def part_rows(fold, part):
        return pl.ds(pl.multiple_of(fold * FOLD + part * PART, PART), PART)

    def bit_rows(fold, part, bit):
        return pl.ds(pl.multiple_of(fold * FOLD + part * PART + bit * BIT, BIT), BIT)

    def tile_of(at):
        fold = at // 8
        row = fold * FOLD + (x + fold * (y - x)) * PART + (y + fold * (x - y)) * BIT + ((at // 2) % 4) * 8
        return pl.ds(pl.multiple_of(row, 8), 8), pl.ds(pl.multiple_of((at % 2) * 128, 128), 128)

    order = [(k, fold) for k in (1, 2, 3, 0) for fold in (0, 1)]
    far_order = [(k, fold) for k in (1, 2, 3) for fold in (0, 1)]

    def order_rows(n):
        k, fold = order[n]
        return part_rows(fold, (first_at[fold] + k) % 4)

    def core_copy(q, n):
        return remote(mine.at[q, order_rows(n)], from_core.at[n], core_send.at[n], core_recv.at[n], sibling)

    def first_copy(q, k, fold):
        rows = part_rows(fold, (first_at[fold] + k) % 4)
        return remote(
            mine.at[q, rows], from_first.at[fold, k - 1], first_send.at[fold, k - 1], first_recv.at[fold, k - 1],
            along[fold][k - 1],
        )

    def second_copy(q, k, fold):
        rows = bit_rows(fold, first_at[fold], (second_at[fold] + k) % 4)
        return remote(
            mine.at[q, rows], from_second.at[fold, k - 1], second_send.at[fold, k - 1], second_recv.at[fold, k - 1],
            along[1 - fold][k - 1],
        )

    def z_copy(q, k):
        rows, columns = tile_of((z + k) % NZ)
        return remote(mine.at[q, rows, columns], from_z.at[k - 1], z_sends.at[k - 1], z_recvs.at[k - 1], z_all[k - 1])

    def zg_copy(q, k, back):
        rows, columns = tile_of((z + NZ - k * back) % NZ)
        tile = out_ref.at[q, rows, columns]
        return remote(tile, tile, zg_send.at[k - 1], zg_recv.at[k - 1], z_all[k - 1])

    def sg_copy(q, k, fold, back):
        bit = out_ref.at[q, bit_rows(fold, first_at[fold], (second_at[fold] + 4 - k * back) % 4)]
        return remote(bit, bit, sg_send.at[fold, k - 1], sg_recv.at[fold, k - 1], along[1 - fold][k - 1])

    def fg_copy(q, k, fold, back):
        part = out_ref.at[q, part_rows(fold, (first_at[fold] + 4 - k * back) % 4)]
        return remote(part, part, fg_send.at[fold, k - 1], fg_recv.at[fold, k - 1], along[fold][k - 1])

    def cg_copy(q, k, fold):
        part = out_ref.at[q, part_rows(fold, (first_at[fold] + 4 - k) % 4)]
        return remote(part, part, cg_send.at[fold, k], cg_recv.at[fold, k], sibling)

    def reduce_first(q):
        for n, (k, fold) in enumerate(order):
            rows = order_rows(n)
            core_copy(q, n).wait_recv()
            mine[q, rows] += from_core[n]
            if k:
                first_copy(q, k, fold).start()

    def reduce_second(q):
        for k, fold in far_order:
            first_copy(q, k, fold).wait_recv()
        for k, fold in order:
            at = (second_at[fold] + k) % 4
            rows = bit_rows(fold, first_at[fold], at)
            near = pl.ds(pl.multiple_of(at * BIT, BIT), BIT)
            mine[q, rows] += from_first[fold, 0, near] + from_first[fold, 1, near] + from_first[fold, 2, near]
            if k:
                second_copy(q, k, fold).start()

    def reduce_z(q):
        for k, fold in far_order:
            second_copy(q, k, fold).wait_recv()
        for fold in (0, 1):
            rows = bit_rows(fold, first_at[fold], second_at[fold])
            mine[q, rows] += from_second[fold, 0] + from_second[fold, 1] + from_second[fold, 2]
        for k in range(1, NZ):
            z_copy(q, k).start()

    def gather_z(q):
        rows, columns = tile_of(z)
        total = mine[q, rows, columns]
        for k in range(1, NZ):
            z_copy(q, k).wait_recv()
            total = total + from_z[k - 1]
        out_ref[q, rows, columns] = total
        for k in range(1, NZ):
            zg_copy(q, k, 0).start()

    def gather_rest(q):
        for k in range(1, NZ):
            zg_copy(q, k, 1).wait_recv()
        for k, fold in far_order:
            sg_copy(q, k, fold, 0).start()
        for k, fold in far_order:
            sg_copy(q, k, fold, 1).wait_recv()
        for k, fold in far_order:
            fg_copy(q, k, fold, 0).start()
        for fold in (0, 1):
            cg_copy(q, 0, fold).start()
        for k, fold in far_order:
            fg_copy(q, k, fold, 1).wait_recv()
            cg_copy(q, k, fold).start()
        for k, fold in far_order:
            first_copy(q, k, fold).wait_send()
            second_copy(q, k, fold).wait_send()
            sg_copy(q, k, fold, 0).wait_send()
            fg_copy(q, k, fold, 0).wait_send()
        for k in range(1, NZ):
            z_copy(q, k).wait_send()
            zg_copy(q, k, 0).wait_send()
        for k, fold in order:
            cg_copy(q, k, fold).wait_send()

    def take_gathered(q):
        for k, fold in order:
            cg_copy(q, k, fold).wait_recv()
        for n in range(len(order)):
            core_copy(q, n).wait_send()

    def on_core(which, action, *given):
        @pl.when(core == which)
        def _():
            action(*given)

    loads[0].wait()
    loads[1].wait()
    unit, inverse = project(cf[...], iw[...])
    unit_c[...] = unit
    inv_c[...] = inverse
    corp[z] = unit.astype(bf16).reshape(2, TOK, E)
    pl.semaphore_wait(barrier, len(greeted))

    def z_send(buf, at, s, e, way, send_sem, recv_sem):
        send(buf.at[at, e], buf.at[at, e], send_sem.at[way, s - 1, e], recv_sem.at[way, s - 1, e], z_peers[way])

    def source(way, s):
        return (z + NZ - s) % NZ if way == 0 else (z + s) % NZ

    def corpus_step(s, work):
        for e in (0, 1):
            for way in (0, 1):
                if s < 8 or e == way:
                    at = source(way, s)
                    arrived(corp.at[at, e], zc_send.at[way, s - 1, e], zc_recv.at[way, s - 1, e], z_peers[way])
                    if s < 7 or (s == 7 and e == way):
                        z_send(corp, at, s + 1, e, way, zc_send, zc_recv)
                if work:
                    work.pop(0)()

    def user_send(at, s, way):
        block = gus.at[at, y_lo]
        send(block, block, zu_send.at[way, s - 1], zu_recv.at[way, s - 1], z_peers[way])
        named = codes.at[at * 2 + y_lo]
        send(named, named, zn_send.at[way, s - 1], zn_recv.at[way, s - 1], z_peers[way])

    def user_step(s):
        for way in (0, 1) if s < 8 else (0,):
            at = source(way, s)
            block = gus.at[at, y_lo]
            named = codes.at[at * 2 + y_lo]
            arrived(block, zu_send.at[way, s - 1], zu_recv.at[way, s - 1], z_peers[way])
            arrived(named, zn_send.at[way, s - 1], zn_recv.at[way, s - 1], z_peers[way])
            if s < 7 or (s == 7 and way == 0):
                user_send(at, s + 1, way)
            send(block, block, yu_send.at[way, s], yu_recv.at[way, s], y_partner)
            send(named, named, yn_send.at[way, s], yn_recv.at[way, s], y_partner)

    def users_handed(s):
        for way in (0, 1) if 0 < s < 8 else (0,):
            block = gus.at[source(way, s), 1 - y_lo]
            named = codes.at[source(way, s) * 2 + 1 - y_lo]
            arrived(block, yu_send.at[way, s], yu_recv.at[way, s], y_partner)
            arrived(named, yn_send.at[way, s], yn_recv.at[way, s], y_partner)

    for e in (0, 1):
        for way in (0, 1):
            z_send(corp, z, 1, e, way, zc_send, zc_recv)
    for load in loads[5:]:
        load.wait()
    code = owner_own[...] * OWN + row_own[...]
    codes[dev] = jnp.concatenate([code, code], axis=0)
    ids[group] = jnp.broadcast_to(ids_own[...], (8, TOK))
    send(codes.at[dev], pair_codes, pair_send, pair_recv, y_partner)

    loads[2].wait()
    loads[3].wait()
    unit, inverse = project(uf[...], uw[...])
    unit_u[...] = unit
    inv_u[...] = inverse
    user_low = unit.astype(bf16)
    cyc[group, 0] = user_low
    gus[z, y_lo] = user_low
    for way in (0, 1):
        user_send(z, 1, way)
    send(gus.at[z, y_lo], gus.at[z, y_lo], yu_send.at[0, 0], yu_recv.at[0, 0], y_partner)
    send(codes.at[dev], codes.at[dev], yn_send.at[0, 0], yn_recv.at[0, 0], y_partner)
    loads[4].wait()
    unit, inverse = project(itf[...], iw[...])
    unit_i[...] = unit
    inv_i[...] = inverse
    item_low = unit.astype(bf16)
    cyc[group, 1] = item_low
    far_group = lax.rem(group + NG // 2, NG)

    def pass_block(at, kind, n, send_sem, recv_sem, device):
        send(cyc.at[at], cyc.at[at], send_sem, recv_sem, device)
        send(ids.at[at], ids.at[at], ids_send.at[kind, n], ids_recv.at[kind, n], device)

    def block_arrived(at, kind, n, send_sem, recv_sem, device):
        arrived(cyc.at[at], send_sem, recv_sem, device)
        arrived(ids.at[at], ids_send.at[kind, n], ids_recv.at[kind, n], device)

    def pass_along_x(at, far):
        for k in range(1, NX):
            pass_block(at, far, k, x_send.at[far, k - 1], x_recv.at[far, k - 1], x_peers[k - 1])

    def pass_to_sibling(at, far, k):
        pass_block(at, 2 + far, k, c_send.at[far, k], c_recv.at[far, k], sibling)

    pass_block(group, 0, 0, yh_send, yh_recv, y_far)
    pass_along_x(group, 0)
    pass_to_sibling(group, 0, 0)

    def group_of(far, k, other):
        row = y_hi + far * (1 - 2 * y_hi)
        return (row * NX + (x + NX - k) % NX) * 2 + core + other * (1 - 2 * core)

    arrived(pair_codes, pair_send, pair_recv, y_partner)
    own_codes, their_codes = codes[dev], pair_codes[...]
    code_row = jnp.concatenate(
        [own_codes[n : n + 1] for n in range(4)] + [their_codes[n : n + 1] for n in range(4)], axis=1
    )
    wide_rows = lax.broadcasted_iota(jnp.int32, (OWN, 2 * NEG), 0)

    def select_from(at):
        hot = (code_row - (at * 2 + y_lo) * OWN == wide_rows).astype(f32).astype(bf16)
        return dot(corp[at].reshape(OWN, E), hot, 0, 0)

    def nothing():
        pass

    def select_more(way, s):
        def piece():
            select[...] += select_from(source(way, s))

        return piece

    code_rows = lax.broadcasted_iota(jnp.int32, (OWN, NEG), 0) + dev * OWN
    ones = jnp.ones((NEG, 128), bf16)

    def count_named(holder):
        named = codes[holder]
        row = jnp.concatenate([named[n : n + 1] for n in range(4)], axis=1)
        counts[holder] = dot((row == code_rows).astype(f32).astype(bf16), ones).astype(bf16)

    def count_piece(s, plane):
        def piece():
            for way in (0, 1) if 0 < s < 8 else (0,):
                count_named(source(way, s) * 2 + plane)

        return piece

    def hand_and_count(s):
        users_handed(s)
        count_piece(s, 1 - y_lo)()

    select[...] = select_from(z)
    count_piece(0, y_lo)()
    for s in range(1, 9):
        work = [nothing, select_more(0, s - 1), nothing, select_more(1, s - 1)] if s > 1 else []
        if s > 1:
            work[0] = count_piece(s - 1, y_lo)
        if s > 2:
            work[2] = functools.partial(hand_and_count, s - 3)
        corpus_step(s, work)
        user_step(s)
        if s == 2:
            block_arrived(far_group, 0, 0, yh_send, yh_recv, y_far)
            pass_along_x(far_group, 1)
            pass_to_sibling(far_group, 1, 0)
        if s in (5, 7):
            far = (s - 5) // 2
            for k in range(1, NX):
                at = group_of(far, k, 0)
                block_arrived(at, far, k, x_send.at[far, k - 1], x_recv.at[far, k - 1], x_peers[k - 1])
                pass_to_sibling(at, far, k)
    select[...] += select_from(source(0, 8))
    sel_out[...] = select[:, NEG:].astype(bf16)
    send(sel_out, sel_in, ys_send, ys_recv, y_partner)

    count_piece(8, y_lo)()
    for s in (6, 7, 8):
        hand_and_count(s)
    for far in (0, 1):
        for k in range(NX):
            block_arrived(group_of(far, k, 1), 2 + far, k, c_send.at[far, k], c_recv.at[far, k], sibling)

    tile_rows = lax.broadcasted_iota(jnp.int32, (TOK, TOK), 0)
    tile_columns = lax.broadcasted_iota(jnp.int32, (TOK, TOK), 1)
    eye = tile_rows == tile_columns

    def to_row(column):
        return jnp.sum(jnp.where(eye, column, 0.0), axis=0, keepdims=True)

    own_ids = ids_own[...].astype(f32)
    ids_column = jnp.sum(jnp.where(eye, own_ids, 0.0), axis=1, keepdims=True)
    user_low = cyc[group, 0]
    item_low = cyc[group, 1]

    wide_columns = lax.broadcasted_iota(jnp.int32, (TOK, QUAD * TOK), 1)
    own_column = lax.broadcasted_iota(jnp.int32, (TOK, QUAD * TOK), 0) + group * TOK

    def side(n, which):
        return cyc[QUAD * n : QUAD * n + QUAD, which].reshape(QUAD * TOK, E)

    def row_of(tiles, n):
        return jnp.concatenate([tiles[QUAD * n + i, 0:1] for i in range(QUAD)], axis=1)

    def diagonal_of(n):
        return wide_columns + n * QUAD * TOK == own_column

    def masks(n):
        diagonal = diagonal_of(n)
        same = row_of(ids, n).astype(f32) == ids_column
        return diagonal, jnp.logical_and(same, jnp.logical_not(diagonal))

    def folded(wide):
        return sum(wide[:, i * TOK : i * TOK + TOK] for i in range(QUAD))

    def forward_piece(n):
        def piece():
            logit = sharpen * dot(user_low, side(n, 1), 1, 1)
            diagonal, hidden = masks(n)
            value = jnp.where(hidden, 0.0, jnp.exp(logit))
            cexp[n] = value
            sums[...] += folded(value)
            own_sums[...] += folded(jnp.where(diagonal, logit, 0.0))

        return piece

    sums[...] = jnp.zeros((TOK, TOK), f32)
    own_sums[...] = jnp.zeros((TOK, TOK), f32)
    for n in range(NG // QUAD):
        forward_piece(n)()
    arrived(sel_in, ys_send, ys_recv, y_partner)
    sample_low = (select[:, :NEG] + sel_in[...].astype(f32)).astype(bf16)
    sample_exp = jnp.exp(sharpen * dot(user_low, sample_low))
    total = jnp.sum(sums[...], axis=1, keepdims=True) + jnp.sum(sample_exp, axis=1, keepdims=True)
    total_row = to_row(total)
    tot_g[group] = jnp.broadcast_to(total_row, (8, TOK))
    tot_d[dev] = jnp.broadcast_to(total_row, (8, TOK))
    for k in range(1, ND):
        send(tot_d.at[dev], tot_d.at[dev], td_send.at[k - 1], td_recv.at[k - 1], dev_peers[k - 1])
    for k in range(1, NG):
        send(tot_g.at[group], tot_g.at[group], tg_send.at[k - 1], tg_recv.at[k - 1], group_peers[k - 1])
    own_logit = jnp.sum(own_sums[...], axis=1, keepdims=True)
    loss_ref[...] = jnp.broadcast_to(to_row(jnp.log(total) - own_logit), (8, TOK))
    inverse_total = 1.0 / total
    sample_grad = (sample_exp * inverse_total * factor).astype(bf16)

    def user_piece(n):
        def piece():
            start = upward[...] if n else dot(sample_grad, sample_low, 1, 1)
            grad = ((cexp[n] * inverse_total - diagonal_of(n).astype(f32)) * factor).astype(bf16)
            upward[...] = start + dot(grad, side(n, 1))

        return piece

    for n in range(NG // QUAD):
        user_piece(n)()
    user_back = unnormalize(unit_u[...], inv_u[...], upward[...])

    def user_part(n):
        rows = order_rows(n)
        mine[0, rows] = dot(uf[:, rows], user_back, 0, 0)
        on_core(1, lambda: core_copy(0, n).start())

    def user_parts(n):
        def piece():
            user_part(2 * n)
            user_part(2 * n + 1)

        return piece

    for n in range(4):
        user_parts(n)()
    for k in range(1, NG):
        arrived(tot_g.at[lax.rem(group + NG - k, NG)], tg_send.at[k - 1], tg_recv.at[k - 1], group_peers[k - 1])

    def item_piece(n):
        def piece():
            users = side(n, 0)
            diagonal, hidden = masks(n)
            value = jnp.where(hidden, 0.0, jnp.exp(sharpen * dot(item_low, users, 1, 1)))
            grad = ((value * (1.0 / row_of(tot_g, n)) - diagonal.astype(f32)) * factor).astype(bf16)
            up = dot(grad, users)
            upward[...] = upward[...] + up if n else up

        return piece

    for n in range(NG // QUAD):
        item_piece(n)()
    item_back = unnormalize(unit_i[...], inv_i[...], upward[...])
    mine[1] = dot(itf[...], item_back, 0, 0)
    on_core(0, reduce_first, 0)
    for k in range(1, ND):
        at = lax.rem(dev + ND - k, ND)
        arrived(tot_d.at[at], td_send.at[k - 1], td_recv.at[k - 1], dev_peers[k - 1])
    owned[...] = jnp.zeros((OWN, E), f32)
    corpus_low = corp[z].reshape(OWN, E)

    def corpus_backward(at):
        users = gus[at].reshape(2 * TOK, E)
        value = jnp.exp(sharpen * dot(corpus_low, users, 1, 1))
        holder = at * 2
        scale = 1.0 / jnp.concatenate([tot_d[holder, 0:1], tot_d[holder + 1, 0:1]], axis=1)
        named = jnp.concatenate([counts[holder], counts[holder + 1]], axis=1).astype(f32)
        return dot((value * scale * factor * named).astype(bf16), users)

    def corpus_piece(*ats):
        def piece():
            owned[...] += sum(corpus_backward(at) for at in ats)

        return piece

    def both(s):
        return source(0, s), source(1, s)

    corpus_piece(z, source(0, 8))()
    for s in range(1, 8):
        corpus_piece(*both(s))()
    owned_back = (owned[...] - unit_c[...] * jnp.sum(unit_c[...] * owned[...], axis=-1, keepdims=True)) * inv_c[...]
    high = owned_back.astype(bf16)
    low = (owned_back - high.astype(f32)).astype(bf16)
    for n in range(len(order)):
        rows = order_rows(n)
        mine[1, rows] += dot(cf[:, rows], high, 0, 0) + dot(cf[:, rows], low, 0, 0)
        on_core(0, lambda: core_copy(1, n).start())
    on_core(1, reduce_first, 1)
    on_core(1, reduce_second, 1)
    on_core(1, reduce_z, 1)
    on_core(1, gather_z, 1)
    on_core(1, gather_rest, 1)
    on_core(0, reduce_second, 0)
    on_core(0, reduce_z, 0)
    on_core(0, gather_z, 0)
    on_core(0, gather_rest, 0)
    on_core(1, take_gathered, 0)
    on_core(0, take_gathered, 1)
    for copy in sends:
        copy.wait_send()


def step(user_feat, item_feat, corpus_feat, user_weight, item_weight, ids, owners, rows):
    dma, vmem = pltpu.SemaphoreType.DMA, pltpu.VMEM
    pairs = lambda *shape: [dma(shape), dma(shape)]
    return pl.pallas_call(
        step_kernel,
        out_shape=[jax.ShapeDtypeStruct((8, TOK), f32), jax.ShapeDtypeStruct((2, WIDE, E), f32)],
        in_specs=[pl.BlockSpec(memory_space=pltpu.HBM)] * 8,
        out_specs=[pl.BlockSpec(memory_space=pltpu.VMEM)] * 2,
        scratch_shapes=[
            vmem((TOK, WIDE), bf16), vmem((TOK, WIDE), bf16), vmem((OWN, WIDE), bf16),
            vmem((WIDE, E), bf16), vmem((WIDE, E), bf16),
            vmem((1, TOK), jnp.int32), vmem((4, 128), jnp.int32), vmem((4, 128), jnp.int32),
            vmem((NZ, 2, TOK, E), bf16), vmem((NZ, 2, TOK, E), bf16), vmem((NG, 2, TOK, E), bf16),
            vmem((NG, 8, 128), jnp.int32), vmem((ND, 8, 128), jnp.int32), vmem((8, 128), jnp.int32),
            vmem((NG, 8, 128), f32), vmem((ND, 8, 128), f32),
            vmem((E, 2 * NEG), f32), vmem((E, NEG), bf16), vmem((E, NEG), bf16), vmem((NG // QUAD, TOK, QUAD * TOK), f32), vmem((ND, OWN, 128), bf16),
            vmem((TOK, TOK), f32), vmem((TOK, TOK), f32),
            vmem((TOK, E), f32), vmem((TOK, E), f32), vmem((OWN, E), f32),
            vmem((TOK, 1), f32), vmem((TOK, 1), f32), vmem((OWN, 1), f32), vmem((TOK, E), f32), vmem((OWN, E), f32),
            vmem((2, WIDE, E), f32), vmem((8, PART, E), f32), vmem((2, 3, PART, E), f32), vmem((2, 3, BIT, E), f32),
            vmem((NZ - 1, 8, 128), f32),
            dma((8,)), *pairs(4, 4), *pairs(2, 8), *pairs(2, 9), *pairs(), *pairs(NG - 1), *pairs(ND - 1),
            *pairs(2, 8, 2), *pairs(2, 8), *pairs(2, 9), *pairs(), *pairs(), *pairs(2, 3), *pairs(2, 4),
            *pairs(8), *pairs(2, 3), *pairs(2, 3), *pairs(NZ - 1), *pairs(NZ - 1), *pairs(2, 3), *pairs(2, 3),
            *pairs(2, 4),
        ],
        compiler_params=pltpu.CompilerParams(
            collective_id=0, has_side_effects=True, vmem_limit_bytes=60 * 1024 * 1024
        ),
        name="step",
    )(user_feat, item_feat, corpus_feat, user_weight, item_weight, ids, owners, rows)


def local(
    user_feat, item_feat, item_ids, corpus_feat, neg_owner, neg_row, user_weight, item_weight
):
    loss, grads = step(
        user_feat, item_feat, corpus_feat, user_weight, item_weight,
        item_ids.reshape(1, TOK), neg_owner.reshape(4, 128), neg_row.reshape(4, 128),
    )
    return loss[0], grads[0], grads[1]


def solution(mesh):
    return jax.shard_map(
        local,
        mesh=mesh,
        in_specs=(
            P(("group", "dev"), None),
            P(("group", "dev"), None),
            P(("group", "dev")),
            P(("group", "dev"), None),
            P(("group", "dev"), None),
            P(("group", "dev")),
            P(),
            P(),
        ),
        out_specs=(P(("group", "dev")), P(), P()),
        check_vma=False,
    )
```

```python
import functools

import jax
import jax.numpy as jnp
from jax import lax
from jax.experimental import pallas as pl
from jax.experimental.pallas import tpu as pltpu
from jax.sharding import PartitionSpec as P

sharpen = 20.0
epsilon = 1e-06
MESH = pl.DeviceIdType.MESH
NX, NY, NZ = 4, 4, 16


def place():
    group, dev = lax.axis_index("group"), lax.axis_index("dev")
    core, x, y_hi = group % 2, (group // 2) % NX, group // (2 * NX)
    z, y_lo = dev // 2, dev % 2
    return core, x, y_hi * 2 + y_lo, z


def device_at(core, x, y, z):
    return (((y // 2) * NX + x) * 2 + core, z * 2 + y % 2)


def greet(partners):
    barrier = pltpu.get_barrier_semaphore()
    for partner in partners:
        pl.semaphore_signal(barrier, inc=1, device_id=partner, device_id_type=MESH)
    pl.semaphore_wait(barrier, len(partners))


def remote(src, dst, send_sem, recv_sem, device):
    return pltpu.make_async_remote_copy(
        src_ref=src, dst_ref=dst, send_sem=send_sem, recv_sem=recv_sem, device_id=device, device_id_type=MESH
    )


TOK, OWN, NEG, WIDE, E = 128, 256, 512, 1024, 256
NG, ND = 16, 32
QUAD = 4
f32, bf16 = jnp.float32, jnp.bfloat16


def dot(left, right, left_dim=1, right_dim=0):
    return lax.dot_general(left, right, (((left_dim,), (right_dim,)), ((), ())), preferred_element_type=f32)


def project(features, weight):
    hidden = dot(features, weight)
    inverse = lax.rsqrt(jnp.sum(hidden * hidden, axis=-1, keepdims=True) + epsilon)
    return hidden * inverse, inverse


def unnormalize(unit, inverse, upstream):
    along = jnp.sum(unit * upstream, axis=-1, keepdims=True)
    return ((upstream - unit * along) * inverse).astype(bf16)


FOLD = 512
PART = 128
BIT = 32


def step_kernel(
    user_feat, item_feat, corpus_feat, user_weight, item_weight, ids_in, owner_in, row_in,
    loss_ref, out_ref,
    uf, itf, cf, uw, iw, ids_own, owner_own, row_own, corp, gus, cyc, ids, codes, pair_codes, tot_g, tot_d,
    select, sel_out, sel_in, cexp, counts, sums, own_sums, unit_u, unit_i, unit_c, inv_u, inv_i, inv_c, upward, owned,
    mine, from_core, from_first, from_second, from_z,
    load_sem, ids_send, ids_recv, zn_send, zn_recv, yn_send, yn_recv, pair_send, pair_recv, tg_send, tg_recv, td_send, td_recv,
    zc_send, zc_recv, zu_send, zu_recv, yu_send, yu_recv, ys_send, ys_recv,
    yh_send, yh_recv, x_send, x_recv, c_send, c_recv,
    core_send, core_recv, first_send, first_recv, second_send, second_recv, z_sends, z_recvs,
    zg_send, zg_recv, sg_send, sg_recv, fg_send, fg_recv, cg_send, cg_recv,
):
    core, x, y, z = place()
    y_hi, y_lo = y // 2, y % 2
    group, dev = lax.axis_index("group"), lax.axis_index("dev")
    factor = sharpen / TOK
    loads = [
        pltpu.make_async_copy(src, dst, load_sem.at[n])
        for n, (src, dst) in enumerate([
            (corpus_feat, cf), (item_weight, iw), (user_feat, uf), (user_weight, uw), (item_feat, itf),
            (ids_in, ids_own), (owner_in, owner_own), (row_in, row_own),
        ])
    ]
    for load in loads:
        load.start()
    group_peers = [(lax.rem(group + k, NG), dev) for k in range(1, NG)]
    dev_peers = [(group, lax.rem(dev + k, ND)) for k in range(1, ND)]
    sibling = device_at(1 - core, x, y, z)
    y_partner = device_at(core, x, y_hi * 2 + 1 - y_lo, z)
    y_far = device_at(core, x, (1 - y_hi) * 2 + y_lo, z)
    x_peers = [device_at(core, (x + k) % NX, y, z) for k in range(1, NX)]
    y_peers = [device_at(core, x, (y + k) % NY, z) for k in range(1, NY)]
    z_all = [device_at(core, x, y, (z + k) % NZ) for k in range(1, NZ)]
    z_peers = [z_all[0], z_all[-1]]
    sends = []

    def send(src, dst, send_sem, recv_sem, device):
        copy = remote(src, dst, send_sem, recv_sem, device)
        copy.start()
        sends.append(copy)

    def arrived(dst, send_sem, recv_sem, device):
        remote(dst, dst, send_sem, recv_sem, device).wait_recv()

    barrier = pltpu.get_barrier_semaphore()
    greeted = [sibling] + x_peers + y_peers + z_peers
    for partner in greeted:
        pl.semaphore_signal(barrier, inc=1, device_id=partner, device_id_type=MESH)

    first_at, second_at = [x, y], [y, x]
    along = [x_peers, y_peers]

    def part_rows(fold, part):
        return pl.ds(pl.multiple_of(fold * FOLD + part * PART, PART), PART)

    def bit_rows(fold, part, bit):
        return pl.ds(pl.multiple_of(fold * FOLD + part * PART + bit * BIT, BIT), BIT)

    def tile_of(at):
        fold = at // 8
        row = fold * FOLD + (x + fold * (y - x)) * PART + (y + fold * (x - y)) * BIT + ((at // 2) % 4) * 8
        return pl.ds(pl.multiple_of(row, 8), 8), pl.ds(pl.multiple_of((at % 2) * 128, 128), 128)

    order = [(k, fold) for k in (1, 2, 3, 0) for fold in (0, 1)]
    far_order = [(k, fold) for k in (1, 2, 3) for fold in (0, 1)]

    def order_rows(n):
        k, fold = order[n]
        return part_rows(fold, (first_at[fold] + k) % 4)

    def core_copy(q, n):
        return remote(mine.at[q, order_rows(n)], from_core.at[n], core_send.at[n], core_recv.at[n], sibling)

    def first_copy(q, k, fold):
        rows = part_rows(fold, (first_at[fold] + k) % 4)
        return remote(
            mine.at[q, rows], from_first.at[fold, k - 1], first_send.at[fold, k - 1], first_recv.at[fold, k - 1],
            along[fold][k - 1],
        )

    def second_copy(q, k, fold):
        rows = bit_rows(fold, first_at[fold], (second_at[fold] + k) % 4)
        return remote(
            mine.at[q, rows], from_second.at[fold, k - 1], second_send.at[fold, k - 1], second_recv.at[fold, k - 1],
            along[1 - fold][k - 1],
        )

    def z_copy(q, k):
        rows, columns = tile_of((z + k) % NZ)
        return remote(mine.at[q, rows, columns], from_z.at[k - 1], z_sends.at[k - 1], z_recvs.at[k - 1], z_all[k - 1])

    def zg_copy(q, k, back):
        rows, columns = tile_of((z + NZ - k * back) % NZ)
        tile = out_ref.at[q, rows, columns]
        return remote(tile, tile, zg_send.at[k - 1], zg_recv.at[k - 1], z_all[k - 1])

    def sg_copy(q, k, fold, back):
        bit = out_ref.at[q, bit_rows(fold, first_at[fold], (second_at[fold] + 4 - k * back) % 4)]
        return remote(bit, bit, sg_send.at[fold, k - 1], sg_recv.at[fold, k - 1], along[1 - fold][k - 1])

    def fg_copy(q, k, fold, back):
        part = out_ref.at[q, part_rows(fold, (first_at[fold] + 4 - k * back) % 4)]
        return remote(part, part, fg_send.at[fold, k - 1], fg_recv.at[fold, k - 1], along[fold][k - 1])

    def cg_copy(q, k, fold):
        part = out_ref.at[q, part_rows(fold, (first_at[fold] + 4 - k) % 4)]
        return remote(part, part, cg_send.at[fold, k], cg_recv.at[fold, k], sibling)

    def reduce_first(q):
        for n, (k, fold) in enumerate(order):
            rows = order_rows(n)
            core_copy(q, n).wait_recv()
            mine[q, rows] += from_core[n]
            if k:
                first_copy(q, k, fold).start()

    def reduce_second(q):
        for k, fold in far_order:
            first_copy(q, k, fold).wait_recv()
        for k, fold in order:
            at = (second_at[fold] + k) % 4
            rows = bit_rows(fold, first_at[fold], at)
            near = pl.ds(pl.multiple_of(at * BIT, BIT), BIT)
            mine[q, rows] += from_first[fold, 0, near] + from_first[fold, 1, near] + from_first[fold, 2, near]
            if k:
                second_copy(q, k, fold).start()

    def reduce_z(q):
        for k, fold in far_order:
            second_copy(q, k, fold).wait_recv()
        for fold in (0, 1):
            rows = bit_rows(fold, first_at[fold], second_at[fold])
            mine[q, rows] += from_second[fold, 0] + from_second[fold, 1] + from_second[fold, 2]
        for k in range(1, NZ):
            z_copy(q, k).start()

    def gather_z(q):
        rows, columns = tile_of(z)
        total = mine[q, rows, columns]
        for k in range(1, NZ):
            z_copy(q, k).wait_recv()
            total = total + from_z[k - 1]
        out_ref[q, rows, columns] = total
        for k in range(1, NZ):
            zg_copy(q, k, 0).start()

    def gather_rest(q):
        for k in range(1, NZ):
            zg_copy(q, k, 1).wait_recv()
        for k, fold in far_order:
            sg_copy(q, k, fold, 0).start()
        for k, fold in far_order:
            sg_copy(q, k, fold, 1).wait_recv()
        for k, fold in far_order:
            fg_copy(q, k, fold, 0).start()
        for fold in (0, 1):
            cg_copy(q, 0, fold).start()
        for k, fold in far_order:
            fg_copy(q, k, fold, 1).wait_recv()
            cg_copy(q, k, fold).start()
        for k, fold in far_order:
            first_copy(q, k, fold).wait_send()
            second_copy(q, k, fold).wait_send()
            sg_copy(q, k, fold, 0).wait_send()
            fg_copy(q, k, fold, 0).wait_send()
        for k in range(1, NZ):
            z_copy(q, k).wait_send()
            zg_copy(q, k, 0).wait_send()
        for k, fold in order:
            cg_copy(q, k, fold).wait_send()

    def take_gathered(q):
        for k, fold in order:
            cg_copy(q, k, fold).wait_recv()
        for n in range(len(order)):
            core_copy(q, n).wait_send()

    def on_core(which, action, *given):
        @pl.when(core == which)
        def _():
            action(*given)

    loads[0].wait()
    loads[1].wait()
    unit, inverse = project(cf[...], iw[...])
    unit_c[...] = unit
    inv_c[...] = inverse
    corp[z] = unit.astype(bf16).reshape(2, TOK, E)
    pl.semaphore_wait(barrier, len(greeted))

    def z_send(buf, at, s, e, way, send_sem, recv_sem):
        send(buf.at[at, e], buf.at[at, e], send_sem.at[way, s - 1, e], recv_sem.at[way, s - 1, e], z_peers[way])

    def source(way, s):
        return (z + NZ - s) % NZ if way == 0 else (z + s) % NZ

    def corpus_step(s, work):
        for e in (0, 1):
            for way in (0, 1):
                if s < 8 or e == way:
                    at = source(way, s)
                    arrived(corp.at[at, e], zc_send.at[way, s - 1, e], zc_recv.at[way, s - 1, e], z_peers[way])
                    if s < 7 or (s == 7 and e == way):
                        z_send(corp, at, s + 1, e, way, zc_send, zc_recv)
                if work:
                    work.pop(0)()

    def user_send(at, s, way):
        block = gus.at[at, y_lo]
        send(block, block, zu_send.at[way, s - 1], zu_recv.at[way, s - 1], z_peers[way])
        named = codes.at[at * 2 + y_lo]
        send(named, named, zn_send.at[way, s - 1], zn_recv.at[way, s - 1], z_peers[way])

    def user_step(s):
        for way in (0, 1) if s < 8 else (0,):
            at = source(way, s)
            block = gus.at[at, y_lo]
            named = codes.at[at * 2 + y_lo]
            arrived(block, zu_send.at[way, s - 1], zu_recv.at[way, s - 1], z_peers[way])
            arrived(named, zn_send.at[way, s - 1], zn_recv.at[way, s - 1], z_peers[way])
            if s < 7 or (s == 7 and way == 0):
                user_send(at, s + 1, way)
            send(block, block, yu_send.at[way, s], yu_recv.at[way, s], y_partner)
            send(named, named, yn_send.at[way, s], yn_recv.at[way, s], y_partner)

    def users_handed(s):
        for way in (0, 1) if 0 < s < 8 else (0,):
            block = gus.at[source(way, s), 1 - y_lo]
            named = codes.at[source(way, s) * 2 + 1 - y_lo]
            arrived(block, yu_send.at[way, s], yu_recv.at[way, s], y_partner)
            arrived(named, yn_send.at[way, s], yn_recv.at[way, s], y_partner)

    for e in (0, 1):
        for way in (0, 1):
            z_send(corp, z, 1, e, way, zc_send, zc_recv)
    for load in loads[5:]:
        load.wait()
    code = owner_own[...] * OWN + row_own[...]
    codes[dev] = jnp.concatenate([code, code], axis=0)
    ids[group] = jnp.broadcast_to(ids_own[...], (8, TOK))
    send(codes.at[dev], pair_codes, pair_send, pair_recv, y_partner)

    loads[2].wait()
    loads[3].wait()
    unit, inverse = project(uf[...], uw[...])
    unit_u[...] = unit
    inv_u[...] = inverse
    user_low = unit.astype(bf16)
    cyc[group, 0] = user_low
    gus[z, y_lo] = user_low
    for way in (0, 1):
        user_send(z, 1, way)
    send(gus.at[z, y_lo], gus.at[z, y_lo], yu_send.at[0, 0], yu_recv.at[0, 0], y_partner)
    send(codes.at[dev], codes.at[dev], yn_send.at[0, 0], yn_recv.at[0, 0], y_partner)
    loads[4].wait()
    unit, inverse = project(itf[...], iw[...])
    unit_i[...] = unit
    inv_i[...] = inverse
    item_low = unit.astype(bf16)
    cyc[group, 1] = item_low
    far_group = lax.rem(group + NG // 2, NG)

    def pass_block(at, kind, n, send_sem, recv_sem, device):
        send(cyc.at[at], cyc.at[at], send_sem, recv_sem, device)
        send(ids.at[at], ids.at[at], ids_send.at[kind, n], ids_recv.at[kind, n], device)

    def block_arrived(at, kind, n, send_sem, recv_sem, device):
        arrived(cyc.at[at], send_sem, recv_sem, device)
        arrived(ids.at[at], ids_send.at[kind, n], ids_recv.at[kind, n], device)

    def pass_along_x(at, far):
        for k in range(1, NX):
            pass_block(at, far, k, x_send.at[far, k - 1], x_recv.at[far, k - 1], x_peers[k - 1])

    def pass_to_sibling(at, far, k):
        pass_block(at, 2 + far, k, c_send.at[far, k], c_recv.at[far, k], sibling)

    pass_block(group, 0, 0, yh_send, yh_recv, y_far)
    pass_along_x(group, 0)
    pass_to_sibling(group, 0, 0)

    def group_of(far, k, other):
        row = y_hi + far * (1 - 2 * y_hi)
        return (row * NX + (x + NX - k) % NX) * 2 + core + other * (1 - 2 * core)

    arrived(pair_codes, pair_send, pair_recv, y_partner)
    own_codes, their_codes = codes[dev], pair_codes[...]
    code_row = jnp.concatenate(
        [own_codes[n : n + 1] for n in range(4)] + [their_codes[n : n + 1] for n in range(4)], axis=1
    )
    wide_rows = lax.broadcasted_iota(jnp.int32, (OWN, 2 * NEG), 0)

    def select_from(at):
        hot = (code_row - (at * 2 + y_lo) * OWN == wide_rows).astype(f32).astype(bf16)
        return dot(corp[at].reshape(OWN, E), hot, 0, 0)

    def nothing():
        pass

    def select_more(way, s):
        def piece():
            select[...] += select_from(source(way, s))

        return piece

    code_rows = lax.broadcasted_iota(jnp.int32, (OWN, NEG), 0) + dev * OWN
    ones = jnp.ones((NEG, 128), bf16)

    def count_named(holder):
        named = codes[holder]
        row = jnp.concatenate([named[n : n + 1] for n in range(4)], axis=1)
        counts[holder] = dot((row == code_rows).astype(f32).astype(bf16), ones).astype(bf16)

    def count_piece(s, plane):
        def piece():
            for way in (0, 1) if 0 < s < 8 else (0,):
                count_named(source(way, s) * 2 + plane)

        return piece

    def hand_and_count(s):
        users_handed(s)
        count_piece(s, 1 - y_lo)()

    select[...] = select_from(z)
    count_piece(0, y_lo)()
    for s in range(1, 9):
        work = [nothing, select_more(0, s - 1), nothing, select_more(1, s - 1)] if s > 1 else []
        if s > 1:
            work[0] = count_piece(s - 1, y_lo)
        if s > 2:
            work[2] = functools.partial(hand_and_count, s - 3)
        corpus_step(s, work)
        user_step(s)
        if s == 2:
            block_arrived(far_group, 0, 0, yh_send, yh_recv, y_far)
            pass_along_x(far_group, 1)
            pass_to_sibling(far_group, 1, 0)
        if s in (5, 7):
            far = (s - 5) // 2
            for k in range(1, NX):
                at = group_of(far, k, 0)
                block_arrived(at, far, k, x_send.at[far, k - 1], x_recv.at[far, k - 1], x_peers[k - 1])
                pass_to_sibling(at, far, k)
    select[...] += select_from(source(0, 8))
    sel_out[...] = select[:, NEG:].astype(bf16)
    send(sel_out, sel_in, ys_send, ys_recv, y_partner)

    count_piece(8, y_lo)()
    for s in (6, 7, 8):
        hand_and_count(s)
    for far in (0, 1):
        for k in range(NX):
            block_arrived(group_of(far, k, 1), 2 + far, k, c_send.at[far, k], c_recv.at[far, k], sibling)

    tile_rows = lax.broadcasted_iota(jnp.int32, (TOK, TOK), 0)
    tile_columns = lax.broadcasted_iota(jnp.int32, (TOK, TOK), 1)
    eye = tile_rows == tile_columns

    def to_row(column):
        return jnp.sum(jnp.where(eye, column, 0.0), axis=0, keepdims=True)

    own_ids = ids_own[...].astype(f32)
    ids_column = jnp.sum(jnp.where(eye, own_ids, 0.0), axis=1, keepdims=True)
    user_low = cyc[group, 0]
    item_low = cyc[group, 1]

    wide_columns = lax.broadcasted_iota(jnp.int32, (TOK, QUAD * TOK), 1)
    own_column = lax.broadcasted_iota(jnp.int32, (TOK, QUAD * TOK), 0) + group * TOK

    def side(n, which):
        return cyc[QUAD * n : QUAD * n + QUAD, which].reshape(QUAD * TOK, E)

    def row_of(tiles, n):
        return jnp.concatenate([tiles[QUAD * n + i, 0:1] for i in range(QUAD)], axis=1)

    def diagonal_of(n):
        return wide_columns + n * QUAD * TOK == own_column

    def masks(n):
        diagonal = diagonal_of(n)
        same = row_of(ids, n).astype(f32) == ids_column
        return diagonal, jnp.logical_and(same, jnp.logical_not(diagonal))

    def folded(wide):
        return sum(wide[:, i * TOK : i * TOK + TOK] for i in range(QUAD))

    def forward_piece(n):
        def piece():
            logit = sharpen * dot(user_low, side(n, 1), 1, 1)
            diagonal, hidden = masks(n)
            value = jnp.where(hidden, 0.0, jnp.exp(logit))
            cexp[n] = value
            sums[...] += folded(value)
            own_sums[...] += folded(jnp.where(diagonal, logit, 0.0))

        return piece

    sums[...] = jnp.zeros((TOK, TOK), f32)
    own_sums[...] = jnp.zeros((TOK, TOK), f32)
    for n in range(NG // QUAD):
        forward_piece(n)()
    arrived(sel_in, ys_send, ys_recv, y_partner)
    sample_low = (select[:, :NEG] + sel_in[...].astype(f32)).astype(bf16)
    sample_exp = jnp.exp(sharpen * dot(user_low, sample_low))
    total = jnp.sum(sums[...], axis=1, keepdims=True) + jnp.sum(sample_exp, axis=1, keepdims=True)
    total_row = to_row(total)
    tot_g[group] = jnp.broadcast_to(total_row, (8, TOK))
    tot_d[dev] = jnp.broadcast_to(total_row, (8, TOK))
    for k in range(1, ND):
        send(tot_d.at[dev], tot_d.at[dev], td_send.at[k - 1], td_recv.at[k - 1], dev_peers[k - 1])
    for k in range(1, NG):
        send(tot_g.at[group], tot_g.at[group], tg_send.at[k - 1], tg_recv.at[k - 1], group_peers[k - 1])
    own_logit = jnp.sum(own_sums[...], axis=1, keepdims=True)
    loss_ref[...] = to_row(jnp.log(total) - own_logit)
    inverse_total = 1.0 / total
    sample_grad = (sample_exp * inverse_total * factor).astype(bf16)

    def user_piece(n):
        def piece():
            start = upward[...] if n else dot(sample_grad, sample_low, 1, 1)
            grad = ((cexp[n] * inverse_total - diagonal_of(n).astype(f32)) * factor).astype(bf16)
            upward[...] = start + dot(grad, side(n, 1))

        return piece

    for n in range(NG // QUAD):
        user_piece(n)()
    user_back = unnormalize(unit_u[...], inv_u[...], upward[...])

    def user_part(n):
        rows = order_rows(n)
        mine[0, rows] = dot(uf[:, rows], user_back, 0, 0)
        on_core(1, lambda: core_copy(0, n).start())

    def user_parts(n):
        def piece():
            user_part(2 * n)
            user_part(2 * n + 1)

        return piece

    for n in range(4):
        user_parts(n)()
    for k in range(1, NG):
        arrived(tot_g.at[lax.rem(group + NG - k, NG)], tg_send.at[k - 1], tg_recv.at[k - 1], group_peers[k - 1])

    def item_piece(n):
        def piece():
            users = side(n, 0)
            diagonal, hidden = masks(n)
            value = jnp.where(hidden, 0.0, jnp.exp(sharpen * dot(item_low, users, 1, 1)))
            grad = ((value * (1.0 / row_of(tot_g, n)) - diagonal.astype(f32)) * factor).astype(bf16)
            up = dot(grad, users)
            upward[...] = upward[...] + up if n else up

        return piece

    for n in range(NG // QUAD):
        item_piece(n)()
    item_back = unnormalize(unit_i[...], inv_i[...], upward[...])
    mine[1] = dot(itf[...], item_back, 0, 0)
    on_core(0, reduce_first, 0)
    for k in range(1, ND):
        at = lax.rem(dev + ND - k, ND)
        arrived(tot_d.at[at], td_send.at[k - 1], td_recv.at[k - 1], dev_peers[k - 1])
    owned[...] = jnp.zeros((OWN, E), f32)
    corpus_low = corp[z].reshape(OWN, E)

    def corpus_backward(at):
        users = gus[at].reshape(2 * TOK, E)
        value = jnp.exp(sharpen * dot(corpus_low, users, 1, 1))
        holder = at * 2
        scale = 1.0 / jnp.concatenate([tot_d[holder, 0:1], tot_d[holder + 1, 0:1]], axis=1)
        named = jnp.concatenate([counts[holder], counts[holder + 1]], axis=1).astype(f32)
        return dot((value * scale * factor * named).astype(bf16), users)

    def corpus_piece(*ats):
        def piece():
            owned[...] += sum(corpus_backward(at) for at in ats)

        return piece

    def both(s):
        return source(0, s), source(1, s)

    corpus_piece(z, source(0, 8))()
    for s in range(1, 8):
        corpus_piece(*both(s))()
    owned_back = (owned[...] - unit_c[...] * jnp.sum(unit_c[...] * owned[...], axis=-1, keepdims=True)) * inv_c[...]
    high = owned_back.astype(bf16)
    low = (owned_back - high.astype(f32)).astype(bf16)
    for n in range(len(order)):
        rows = order_rows(n)
        mine[1, rows] += dot(cf[:, rows], high, 0, 0) + dot(cf[:, rows], low, 0, 0)
        on_core(0, lambda: core_copy(1, n).start())
    on_core(1, reduce_first, 1)
    on_core(1, reduce_second, 1)
    on_core(1, reduce_z, 1)
    on_core(1, gather_z, 1)
    on_core(1, gather_rest, 1)
    on_core(0, reduce_second, 0)
    on_core(0, reduce_z, 0)
    on_core(0, gather_z, 0)
    on_core(0, gather_rest, 0)
    on_core(1, take_gathered, 0)
    on_core(0, take_gathered, 1)
    for copy in sends:
        copy.wait_send()


def step(user_feat, item_feat, corpus_feat, user_weight, item_weight, ids, owners, rows):
    dma, vmem = pltpu.SemaphoreType.DMA, pltpu.VMEM
    pairs = lambda *shape: [dma(shape), dma(shape)]
    return pl.pallas_call(
        step_kernel,
        out_shape=[jax.ShapeDtypeStruct((1, TOK), f32), jax.ShapeDtypeStruct((2, WIDE, E), f32)],
        in_specs=[pl.BlockSpec(memory_space=pltpu.HBM)] * 8,
        out_specs=[pl.BlockSpec(memory_space=pltpu.VMEM)] * 2,
        scratch_shapes=[
            vmem((TOK, WIDE), bf16), vmem((TOK, WIDE), bf16), vmem((OWN, WIDE), bf16),
            vmem((WIDE, E), bf16), vmem((WIDE, E), bf16),
            vmem((1, TOK), jnp.int32), vmem((4, 128), jnp.int32), vmem((4, 128), jnp.int32),
            vmem((NZ, 2, TOK, E), bf16), vmem((NZ, 2, TOK, E), bf16), vmem((NG, 2, TOK, E), bf16),
            vmem((NG, 8, 128), jnp.int32), vmem((ND, 8, 128), jnp.int32), vmem((8, 128), jnp.int32),
            vmem((NG, 8, 128), f32), vmem((ND, 8, 128), f32),
            vmem((E, 2 * NEG), f32), vmem((E, NEG), bf16), vmem((E, NEG), bf16), vmem((NG // QUAD, TOK, QUAD * TOK), f32), vmem((ND, OWN, 128), bf16),
            vmem((TOK, TOK), f32), vmem((TOK, TOK), f32),
            vmem((TOK, E), f32), vmem((TOK, E), f32), vmem((OWN, E), f32),
            vmem((TOK, 1), f32), vmem((TOK, 1), f32), vmem((OWN, 1), f32), vmem((TOK, E), f32), vmem((OWN, E), f32),
            vmem((2, WIDE, E), f32), vmem((8, PART, E), f32), vmem((2, 3, PART, E), f32), vmem((2, 3, BIT, E), f32),
            vmem((NZ - 1, 8, 128), f32),
            dma((8,)), *pairs(4, 4), *pairs(2, 8), *pairs(2, 9), *pairs(), *pairs(NG - 1), *pairs(ND - 1),
            *pairs(2, 8, 2), *pairs(2, 8), *pairs(2, 9), *pairs(), *pairs(), *pairs(2, 3), *pairs(2, 4),
            *pairs(8), *pairs(2, 3), *pairs(2, 3), *pairs(NZ - 1), *pairs(NZ - 1), *pairs(2, 3), *pairs(2, 3),
            *pairs(2, 4),
        ],
        compiler_params=pltpu.CompilerParams(
            collective_id=0, has_side_effects=True, vmem_limit_bytes=60 * 1024 * 1024
        ),
        name="step",
    )(user_feat, item_feat, corpus_feat, user_weight, item_weight, ids, owners, rows)


def local(
    user_feat, item_feat, item_ids, corpus_feat, neg_owner, neg_row, user_weight, item_weight
):
    loss, grads = step(
        user_feat, item_feat, corpus_feat, user_weight, item_weight,
        item_ids.reshape(1, TOK), neg_owner.reshape(4, 128), neg_row.reshape(4, 128),
    )
    return loss.reshape(TOK), grads[0], grads[1]


def solution(mesh):
    return jax.shard_map(
        local,
        mesh=mesh,
        in_specs=(
            P(("group", "dev"), None),
            P(("group", "dev"), None),
            P(("group", "dev")),
            P(("group", "dev"), None),
            P(("group", "dev"), None),
            P(("group", "dev")),
            P(),
            P(),
        ),
        out_specs=(P(("group", "dev")), P(), P()),
        check_vma=False,
    )
```
